32 devices in a mesh: dp: 4 (over x, core), ctx: 8 (over z, y).
Axes of the slice: x: 2, y: 2, z: 4, core: 2. Of those that a mesh axis runs over, the one named last changes fastest.
Arguments:
- queries: bfloat16 [4, 1024, 512], P('dp', 'ctx'), may hold values from -6 to 6
- keys: bfloat16 [4, 1024, 512], P('dp', 'ctx'), may hold values from -6 to 6
- values: bfloat16 [4, 1024, 512], P('dp', 'ctx'), may hold values from -6 to 6
- grad_out: bfloat16 [4, 1024, 8192], P('dp', 'ctx'), may hold values from -6 to 6
- out_weight: bfloat16 [512, 8192], P(None, 'ctx'), may hold values from -0.25 to 0.25
- residues: float32 [512, 16], P('ctx'), may hold values from -0.25 to 0.25
- decays: float32 [512, 16], P('ctx'), may hold values from 4.8828126e-05 to 0.1
Outputs:
- grad_queries: bfloat16 [4, 1024, 512], P('dp', None, 'ctx')
- grad_keys: bfloat16 [4, 1024, 512], P('dp', None, 'ctx')
- grad_values: bfloat16 [4, 1024, 512], P('dp', None, 'ctx')
- grad_weight: float32 [512, 8192], P(None, 'ctx')
- grad_residues: float32 [512, 16], P('ctx')
- grad_decays: float32 [512, 16], P('ctx')
The draws below stay inside these ranges and needn't reach their ends.
All inputs are finite; a program needn't handle non-finite values.
Results may differ from the reference program's by a relative error of at most 0.017.
Values may be sent and summed in bfloat16 or wider, within the bound.
A program may use at most 128 MiB of HBM per device.

```python
import math
import jax
import jax.numpy as jnp
from jax import lax

D = 8192
C = 512
ORDER = 16
SEQ = 1024
BATCH = 4
N_CTX = 8


def level_of(key, dims, split, least, high):
    def one(dim, shards_of):
        draws = jax.random.uniform(jax.random.fold_in(jax.random.fold_in(key, 6), dim), (shards_of,), jnp.float32, least / len(split), high / len(split))
        return jnp.repeat(jnp.exp(draws), dims[dim] // shards_of).reshape((-1,) + (1,) * (len(dims) - dim - 1))

    gain = one(*split[0])
    for cut in split[1:]:
        gain = gain * one(*cut)
    return gain


def normal_values(stream_key, extent, deviation, reach, pieces=(), dtype=jnp.bfloat16):
    level = level_of(stream_key, extent, pieces, -0.22, 0.18) if pieces else 1.0
    array = jax.random.normal(stream_key, extent, jnp.float32) * deviation * level
    return jnp.minimum(jnp.maximum(array, -reach), reach).astype(dtype)


def setup_inputs(seed: int = 0) -> dict:
    arg_keys = jax.random.split(jax.random.key(seed), 8)
    queries = normal_values(arg_keys[0], (BATCH, SEQ, C), 1.0, 6.0, ((0, 4), (1, 8)))
    keys = normal_values(arg_keys[1], (BATCH, SEQ, C), 1.0, 6.0, ((0, 4), (1, 8)))
    values = normal_values(arg_keys[2], (BATCH, SEQ, C), 1.0, 6.0, ((0, 4), (1, 8)))
    grad_out = normal_values(arg_keys[3], (BATCH, SEQ, D), 1.0, 6.0, ((0, 4), (1, 8)))
    out_weight = normal_values(arg_keys[4], (C, D), C ** -0.5, 0.25, ((1, 8),))
    residues = normal_values(arg_keys[5], (C, ORDER), (2.0 / (ORDER * SEQ) ** 0.5), 0.25, ((0, 8),), jnp.float32)
    decays = jnp.clip(jnp.exp(math.log(0.1) - 7.624619 * jax.random.uniform(arg_keys[6], (C, ORDER), jnp.float32) ** level_of(arg_keys[6], (C, ORDER), ((0, 8),), -0.2, 0.2)), 4.882812572759576e-05, 0.1)
    return {"queries": queries, "keys": keys, "values": values, "grad_out": grad_out, "out_weight": out_weight, "residues": residues, "decays": decays}


def reference(queries, keys, values, grad_out, out_weight, residues, decays):
    positions = jnp.arange(SEQ).astype(jnp.float32)
    decay_terms = jnp.exp(-decays[None, :, :] * positions[:, None, None])
    filter_taps = jnp.sum(residues[None, :, :] * decay_terms, axis=2)
    length = 2 * SEQ
    filter_freq = jnp.fft.rfft(filter_taps, n=length, axis=0)
    block_width = D // N_CTX

    def one_sequence(carry, items):
        weight_sum, taps_sum = carry
        query_rows, key_rows, value_rows, grad_rows = items

        def add_block(index, total):
            offset = (index * block_width).astype(jnp.int32)
            grad_part = lax.dynamic_slice_in_dim(grad_rows, offset, block_width, 1)
            weight_part = lax.dynamic_slice_in_dim(out_weight, offset, block_width, 1)
            term = jnp.dot(grad_part, weight_part.T, preferred_element_type=jnp.float32).astype(jnp.bfloat16)
            term = lax.optimization_barrier(term)
            return total + term.astype(jnp.float32)

        gated_sum = lax.fori_loop(0, N_CTX, add_block, jnp.zeros((SEQ, C), jnp.float32))
        grad_gated = gated_sum.astype(jnp.bfloat16)
        query_full = query_rows.astype(jnp.float32)
        key_full = key_rows.astype(jnp.float32)
        value_full = value_rows.astype(jnp.float32)
        product = key_full * value_full
        prod_freq = jnp.fft.rfft(product, n=length, axis=0)
        conv_out = jnp.fft.irfft(prod_freq * filter_freq, n=length, axis=0)[:SEQ]
        gated = (query_full * conv_out).astype(jnp.bfloat16)
        grad_queries = (grad_gated.astype(jnp.float32) * conv_out).astype(jnp.bfloat16)
        grad_conv = grad_gated.astype(jnp.float32) * query_full
        grad_freq = jnp.fft.rfft(grad_conv, n=length, axis=0)
        grad_product = jnp.fft.irfft(jnp.conj(filter_freq) * grad_freq, n=length, axis=0)[:SEQ]
        grad_taps = jnp.fft.irfft(jnp.conj(prod_freq) * grad_freq, n=length, axis=0)[:SEQ]
        grad_keys = (grad_product * value_full).astype(jnp.bfloat16)
        grad_values = (grad_product * key_full).astype(jnp.bfloat16)
        weight_sum = weight_sum + jnp.dot(gated.T, grad_rows, preferred_element_type=jnp.float32)
        taps_sum = taps_sum + grad_taps
        return (weight_sum, taps_sum), (grad_queries, grad_keys, grad_values)

    start = (jnp.zeros((C, D), jnp.float32), jnp.zeros((SEQ, C), jnp.float32))
    (grad_weight, taps_sum), (grad_queries, grad_keys, grad_values) = lax.scan(
        one_sequence, start, (queries, keys, values, grad_out))
    grad_residues = jnp.sum(taps_sum[:, :, None] * decay_terms, axis=0)
    grad_decays = -residues * jnp.sum((taps_sum * positions[:, None])[:, :, None] * decay_terms, axis=0)
    return grad_queries, grad_keys, grad_values, grad_weight, grad_residues, grad_decays
```

```python
import functools
import math

import jax
import jax.numpy as jnp
from jax import lax
from jax.experimental import pallas as pl
from jax.experimental.pallas import tpu as pltpu
from jax.sharding import PartitionSpec as P

FFT_COLS = 128


HIGHEST = lax.Precision.HIGHEST


def fourier_tables(fft_rows, fft_cols):
    total = fft_rows * fft_cols
    row_index = jnp.arange(fft_rows, dtype=jnp.int32)
    col_index = jnp.arange(fft_cols, dtype=jnp.int32)
    first = (row_index[:, None] * row_index[None, :] % fft_rows).astype(jnp.float32) * (
        2.0 * math.pi / fft_rows
    )
    twist = (row_index[:, None] * col_index[None, :] % total).astype(jnp.float32) * (
        2.0 * math.pi / total
    )
    second = (col_index[:, None] * col_index[None, :] % fft_cols).astype(jnp.float32) * (
        2.0 * math.pi / fft_cols
    )
    return (
        (jnp.cos(first), -jnp.sin(first)),
        (jnp.cos(twist), -jnp.sin(twist)),
        (jnp.cos(second), -jnp.sin(second)),
    )


def complex_product(left_re, left_im, right_re, right_im):
    return (left_re * right_re - left_im * right_im, left_re * right_im + left_im * right_re)


def apply_middle(table_re, table_im, data_re):

    def single(table, data):
        return jnp.einsum("kn,cnm->ckm", table, data, precision=HIGHEST)

    return (single(table_re, data_re), single(table_im, data_re))


def apply_last(table_re, table_im, data_re, data_im):

    def single(data, table):
        return jnp.einsum("ckm,mj->ckj", data, table, precision=HIGHEST)

    return (
        single(data_re, table_re) - single(data_im, table_im),
        single(data_im, table_re) + single(data_re, table_im),
    )


def forward_transform(signal, tables):
    (first_re, first_im), (twist_re, twist_im), (second_re, second_im) = tables
    section_re, section_im = apply_middle(first_re, first_im, signal)
    section_re, section_im = complex_product(section_re, section_im, twist_re, twist_im)
    return apply_last(second_re, second_im, section_re, section_im)


def inverse_transform(spec_re, spec_im, tables):
    (first_re, first_im), (twist_re, twist_im), (second_re, second_im) = tables
    section_re, section_im = apply_last(second_re, -second_im, spec_re, spec_im)
    section_re, section_im = complex_product(section_re, section_im, twist_re, -twist_im)
    result = jnp.einsum("kn,cnm->ckm", first_re, section_re, precision=HIGHEST) + jnp.einsum(
        "kn,cnm->ckm", first_im, section_im, precision=HIGHEST
    )
    total = first_re.shape[0] * second_re.shape[0]
    return result / float(total)


def padded_grid(signal, fft_rows, fft_cols):
    channels, seq_len = signal.shape
    padded = jnp.concatenate(
        [signal, jnp.zeros((channels, fft_rows * fft_cols - seq_len), jnp.float32)], axis=1
    )
    return padded.reshape(channels, fft_rows, fft_cols)


def leading_part(grid, seq_len):
    return grid.reshape(grid.shape[0], -1)[:, :seq_len]


def channels_first(block):
    return block[0].astype(jnp.float32).T


def rounded_sum(terms):
    rounded = lax.optimization_barrier(terms.astype(jnp.bfloat16))
    return jnp.sum(rounded.astype(jnp.float32), axis=0)


def body(queries, keys, values, grad_out, out_weight, residues, decays):
    channels = out_weight.shape[0]
    block_width = out_weight.shape[1]
    tok_rows = grad_out.shape[1]
    grad_cols = lax.all_to_all(grad_out, "ctx", split_axis=2, concat_axis=1, tiled=True)
    shard_piece = lax.all_gather(out_weight, "ctx", axis=1, tiled=True)
    blocks = shard_piece.shape[1] // block_width
    partial_value = grad_out[0]
    partial_value = partial_value.reshape(tok_rows, blocks, block_width)
    weight_part = shard_piece.reshape(channels, blocks, block_width)
    terms = jnp.einsum(
        "tks,cks->ktc", partial_value, weight_part, preferred_element_type=jnp.float32
    )
    gated_sum = rounded_sum(terms)
    grad_gated = gated_sum.astype(jnp.bfloat16)[None]
    query_ch, key_ch, value_ch, gated_grad_ch = (
        lax.all_to_all(queries, "ctx", split_axis=2, concat_axis=1, tiled=True),
        lax.all_to_all(keys, "ctx", split_axis=2, concat_axis=1, tiled=True),
        lax.all_to_all(values, "ctx", split_axis=2, concat_axis=1, tiled=True),
        lax.all_to_all(grad_gated, "ctx", split_axis=2, concat_axis=1, tiled=True),
    )
    grad_gated_full = channels_first(gated_grad_ch)
    seq_len = query_ch.shape[1]
    fft_rows = 2 * seq_len // FFT_COLS
    tables = fourier_tables(fft_rows, FFT_COLS)
    query_full = channels_first(query_ch)
    key_full = channels_first(key_ch)
    value_full = channels_first(value_ch)
    positions = jnp.arange(seq_len).astype(jnp.float32)
    decay_terms = jnp.exp(-decays[:, :, None] * positions[None, None, :])
    filter_taps = jnp.sum(residues[:, :, None] * decay_terms, axis=1)
    product = key_full * value_full
    grad_conv = grad_gated_full * query_full
    prod_re, prod_im = forward_transform(padded_grid(product, fft_rows, FFT_COLS), tables)
    taps_re, taps_im = forward_transform(padded_grid(filter_taps, fft_rows, FFT_COLS), tables)
    grad_re, grad_im = forward_transform(padded_grid(grad_conv, fft_rows, FFT_COLS), tables)
    conv_out = leading_part(
        inverse_transform(*complex_product(prod_re, prod_im, taps_re, taps_im), tables), seq_len
    )
    grad_product = leading_part(
        inverse_transform(*complex_product(taps_re, -taps_im, grad_re, grad_im), tables), seq_len
    )
    grad_taps = leading_part(
        inverse_transform(*complex_product(prod_re, -prod_im, grad_re, grad_im), tables), seq_len
    )
    gated = (query_full * conv_out).T.astype(jnp.bfloat16)[None]
    grad_queries = (grad_gated_full * conv_out).T.astype(jnp.bfloat16)[None]
    grad_keys = (grad_product * value_full).T.astype(jnp.bfloat16)[None]
    grad_values = (grad_product * key_full).T.astype(jnp.bfloat16)[None]
    partial_value = lax.dot_general(
        lax.all_gather(gated, "ctx", axis=2, tiled=True)[0],
        grad_cols[0],
        (((0,), (0,)), ((), ())),
        preferred_element_type=jnp.float32,
    )
    grad_weight = partial_value
    grad_residues = jnp.sum(grad_taps[:, None, :] * decay_terms, axis=2)
    grad_decays = -residues * jnp.sum(
        (grad_taps * positions[None, :])[:, None, :] * decay_terms, axis=2
    )
    grad_weight, grad_residues, grad_decays = (
        lax.psum(grad_weight.astype(jnp.bfloat16), "dp").astype(jnp.float32),
        lax.psum(grad_residues.astype(jnp.bfloat16), "dp").astype(jnp.float32),
        lax.psum(grad_decays.astype(jnp.bfloat16), "dp").astype(jnp.float32),
    )
    return (grad_queries, grad_keys, grad_values, grad_weight, grad_residues, grad_decays)

LANES = 128
MESH = pl.DeviceIdType.MESH
F32 = jnp.float32
BF16 = jnp.bfloat16


def dot_nt(left, right):
    return lax.dot_general(left, right, (((1,), (1,)), ((), ())), preferred_element_type=F32)


def split_rows(data):
    high = data.astype(BF16)
    low = (data - high.astype(F32)).astype(BF16)
    return jnp.concatenate([high, low], axis=0)


def fused_kernel(
    n_dp, n_ctx,
    q_ref, k_ref, v_ref, go_ref, w_ref, dec_ref, res_ref, res_plain_ref,
    gq_ref, gk_ref, gv_ref, dw_ref, par_ref,
    qkv_send, qkv_recv, gcols, wbuf, toep, etab, prod, conv, gconv, gprod,
    gat_send, gat_all, gg_acc, gg_send, gg_recv, ggt_send, ggt_recv,
    dwp, dwy, dwz, dwf, red, red_send, red_recv,
    q_ss, q_rs, g_ss, g_rs, w_ss, w_rs, a_ss, a_rs, b_ss, b_rs, c_ss, c_rs, t_ss, t_rs,
    y_ss, y_rs, z_ss, z_rs, f_ss, f_rs, r_ss, r_rs, loc_sem,
):
    me_d = lax.axis_index("dp")
    me_c = lax.axis_index("ctx")
    chans = q_ref.shape[2]
    mine = chans // n_ctx
    width = gcols.shape[2]
    block = width * n_dp
    order = dec_ref.shape[1]
    half = n_ctx // 2
    side = lax.rem(me_c, 2)
    partner = me_c + 1 - 2 * side
    ctx_peers = [lax.rem(me_c + s, n_ctx) for s in range(1, n_ctx)]
    dp_peers = [lax.rem(me_d + s, n_dp) for s in range(1, n_dp)]
    line_peers = [lax.rem(me_c + 2 * s, n_ctx) for s in range(1, half)]

    def remote(src, dst, ss, rs, **to):
        return pltpu.make_async_remote_copy(
            src_ref=src, dst_ref=dst, send_sem=ss, recv_sem=rs, device_id=to, device_id_type=MESH
        )

    def rows(index, size):
        return pl.ds(pl.multiple_of(index * size, size), size)

    barrier = pltpu.get_barrier_semaphore()
    for peer in ctx_peers:
        pl.semaphore_signal(barrier, inc=1, device_id={"ctx": peer}, device_id_type=MESH)
    for peer in dp_peers:
        pl.semaphore_signal(barrier, inc=1, device_id={"dp": peer}, device_id_type=MESH)

    for part, ref in enumerate((q_ref, k_ref, v_ref)):
        for at in range(0, chans, LANES):
            qkv_send[part, at : at + LANES, :] = ref[0, :, at : at + LANES].astype(F32).T.astype(BF16)
    pl.semaphore_wait(barrier, n_ctx - 1 + n_dp - 1)

    q_copies = [
        remote(qkv_send.at[:, rows(peer, mine), :], qkv_recv.at[me_c], q_ss.at[i], q_rs.at[i], ctx=peer)
        for i, peer in enumerate(ctx_peers)
    ]
    for copy in q_copies:
        copy.start()
    qkv_recv[me_c] = qkv_send[:, rows(me_c, mine), :]

    def cols_copy(i, peer, k):
        return remote(
            go_ref.at[0, :, rows(k * n_dp + peer, width)],
            gcols.at[k, rows(me_d, LANES), :],
            g_ss.at[i, k], g_rs.at[i, k], dp=peer,
        )

    def cols_own(k):
        return pltpu.make_async_copy(
            go_ref.at[0, :, rows(k * n_dp + me_d, width)], gcols.at[k, rows(me_d, LANES), :], loc_sem.at[k]
        )

    for k in range(n_ctx):
        for i, peer in enumerate(dp_peers):
            cols_copy(i, peer, k).start()
        cols_own(k).start()

    own_w = pltpu.make_async_copy(w_ref.at[:, rows(me_d, width)], wbuf.at[me_c], loc_sem.at[n_ctx])
    own_w.start()
    w_own = w_ref.at[:, rows(me_d, width)]
    w_copies = [
        remote(w_own, wbuf.at[me_c], w_ss.at[i], w_rs.at[i], ctx=peer)
        for i, peer in enumerate(line_peers + [partner])
    ]
    for copy in w_copies:
        copy.start()

    lane = lax.broadcasted_iota(jnp.int32, (order, LANES), 1).astype(F32)
    upper = lax.broadcasted_iota(jnp.int32, (LANES, LANES), 1) >= lax.broadcasted_iota(
        jnp.int32, (LANES, LANES), 0
    )
    block_row = lax.broadcasted_iota(jnp.int32, (n_ctx, LANES), 0)

    def tables(c, carry):
        rate = dec_ref[c]
        weight = res_ref[c]
        taps = []
        for m in range(n_ctx):
            at = lane + float(m * LANES)
            value = jnp.exp(-rate * at)
            timed = value * at
            etab[c, :, m * LANES : (m + 1) * LANES] = jnp.concatenate(
                [split_rows(value), split_rows(timed)], axis=0
            )
            taps.append(jnp.sum(weight * value, axis=0, keepdims=True))
        wide = jnp.broadcast_to(jnp.concatenate(taps, axis=1), (LANES, n_ctx * LANES))
        rolled = pltpu.roll(wide, 0, 1, stride=1, stride_axis=0)
        toep[c, :, 0:LANES] = jnp.where(upper, rolled[:, 0:LANES], 0.0).astype(BF16)
        toep[c, :, LANES:] = rolled[:, LANES:].astype(BF16)
        return carry

    lax.fori_loop(0, mine, tables, 0)

    for copy in q_copies:
        copy.wait()
    for j in range(n_ctx):
        prod[j * mine : (j + 1) * mine, :] = qkv_recv[j, 1].astype(F32) * qkv_recv[j, 2].astype(F32)

    def forward(c, carry):
        both = jnp.dot(split_rows(prod[pl.ds(c, n_ctx, stride=mine), :]), toep[c], preferred_element_type=F32)
        both = both[:n_ctx] + both[n_ctx:]
        total = both[:, 0:LANES]
        for m in range(1, n_ctx):
            moved = pltpu.roll(both[:, m * LANES : (m + 1) * LANES], m, 0)
            total = total + jnp.where(block_row >= m, moved, 0.0)
        conv[pl.ds(c, n_ctx, stride=mine), :] = total
        return carry

    lax.fori_loop(0, mine, forward, 0, unroll=4)

    for j in range(n_ctx):
        gat_send[j] = (qkv_recv[j, 0].astype(F32) * conv[j * mine : (j + 1) * mine, :]).astype(BF16)
    a_copies = [
        remote(
            gat_send.at[peer],
            gat_all.at[rows(me_c, mine), rows(me_d, LANES)],
            a_ss.at[i], a_rs.at[i], ctx=peer,
        )
        for i, peer in enumerate(ctx_peers)
    ]
    for copy in a_copies:
        copy.start()
    gat_all[rows(me_c, mine), rows(me_d, LANES)] = gat_send[me_c]

    forwards = []
    for i, peer in enumerate(line_peers):
        w_copies[i].wait()
        source = lax.rem(me_c + n_ctx - 2 * (i + 1), n_ctx)
        copy = remote(wbuf.at[source], wbuf.at[source], w_ss.at[half + i], w_rs.at[half + i], ctx=partner)
        copy.start()
        forwards.append(copy)

    for copy in a_copies:
        copy.wait()
    b_copies = [
        remote(
            gat_all.at[:, rows(me_d, LANES)], gat_all.at[:, rows(me_d, LANES)],
            b_ss.at[i], b_rs.at[i], dp=peer,
        )
        for i, peer in enumerate(dp_peers)
    ]
    for copy in b_copies:
        copy.start()

    for k in range(n_ctx):
        for i, peer in enumerate(dp_peers):
            cols_copy(i, peer, k).wait()
        cols_own(k).wait()
    own_w.wait()
    w_copies[half - 1].wait()
    for copy in forwards:
        copy.wait()

    gg_acc[...] = jnp.zeros_like(gg_acc)

    def terms(k, carry):
        gg_acc[...] += dot_nt(wbuf[k], gcols[k])
        return carry

    lax.fori_loop(0, n_ctx, terms, 0)
    gg_send[...] = gg_acc[...].astype(BF16)
    c_copies = [
        remote(gg_send.at[:, rows(peer, LANES)], gg_recv.at[me_d], c_ss.at[i], c_rs.at[i], dp=peer)
        for i, peer in enumerate(dp_peers)
    ]
    for copy in c_copies:
        copy.start()

    for copy in b_copies:
        copy.wait()

    def weight_block(k):
        return jnp.dot(gat_all[...], gcols[k], preferred_element_type=F32)

    y_copies = []
    for z in range(half):
        k = 2 * z + 1 - side
        dwp[k] = weight_block(k).astype(BF16)
        copy = remote(dwp.at[k], dwy.at[z], y_ss.at[z], y_rs.at[z], ctx=partner)
        copy.start()
        y_copies.append(copy)

    for copy in c_copies:
        copy.wait()
    gg_recv[me_d] = gg_send[:, rows(me_d, LANES)]
    total = gg_recv[0].astype(F32)
    for d in range(1, n_dp):
        total = total + gg_recv[d].astype(F32)
    ggt_send[...] = total.astype(BF16)
    t_copies = [
        remote(ggt_send.at[rows(peer, mine), :], ggt_recv.at[me_c], t_ss.at[i], t_rs.at[i], ctx=peer)
        for i, peer in enumerate(ctx_peers)
    ]
    for copy in t_copies:
        copy.start()
    ggt_recv[me_c] = ggt_send[rows(me_c, mine), :]

    def own_blocks(z, carry):
        k = 2 * z + side
        dwp[k] = weight_block(k).astype(BF16)
        return carry

    lax.fori_loop(0, half, own_blocks, 0)
    for copy in y_copies:
        copy.wait()
    z_copies = []
    for i, peer in enumerate(line_peers):
        dwp[peer] = (dwp[peer].astype(F32) + dwy[peer // 2].astype(F32)).astype(BF16)
        copy = remote(dwp.at[peer], dwz.at[i], z_ss.at[i], z_rs.at[i], ctx=peer)
        copy.start()
        z_copies.append(copy)

    for copy in t_copies:
        copy.wait()
    for j in range(n_ctx):
        part = slice(j * mine, (j + 1) * mine)
        gated_grad = ggt_recv[j].astype(F32)
        gconv[part, :] = gated_grad * qkv_recv[j, 0].astype(F32)
        gq_ref[j] = (gated_grad * conv[part, :]).astype(BF16)

    def window(c):
        grad = gconv[pl.ds(c, n_ctx, stride=mine), :]
        tiles = [grad]
        for m in range(1, n_ctx):
            moved = pltpu.roll(grad, n_ctx - m, 0)
            tiles.append(jnp.where(block_row < n_ctx - m, moved, 0.0))
        return jnp.concatenate(tiles, axis=1)

    def backward(c, carry):
        both = dot_nt(split_rows(window(c)), toep[c])
        gprod[pl.ds(c, n_ctx, stride=mine), :] = both[:n_ctx] + both[n_ctx:]
        return carry

    def lags(c, carry):
        left = prod[pl.ds(c, n_ctx, stride=mine), :].astype(BF16)
        outer = lax.dot_general(
            left, window(c).astype(BF16), (((0,), (0,)), ((), ())), preferred_element_type=F32
        )
        outer = jnp.concatenate(
            [jnp.where(upper, outer[:, 0:LANES], 0.0).astype(BF16), outer[:, LANES:].astype(BF16)], axis=1
        )
        sums = dot_nt(etab[c], outer)
        plain = sums[0:order] + sums[order : 2 * order]
        timed = sums[2 * order : 3 * order] + sums[3 * order :]
        grown = jnp.exp(dec_ref[c] * lane)
        red[c, 0:order, :] = plain * grown
        red[c, order:, :] = (timed - lane * plain) * grown
        return carry

    lax.fori_loop(0, mine, backward, 0, unroll=4)
    for copy in z_copies:
        copy.wait()
    last = dwp[me_c].astype(F32) + dwy[me_c // 2].astype(F32)
    for i in range(half - 1):
        last = last + dwz[i].astype(F32)
    dwf[:, rows(me_d, width)] = last.astype(BF16)
    f_copies = [
        remote(
            dwf.at[:, rows(me_d, width)], dwf.at[:, rows(me_d, width)], f_ss.at[i], f_rs.at[i], dp=peer
        )
        for i, peer in enumerate(dp_peers)
    ]
    for copy in f_copies:
        copy.start()

    lax.fori_loop(0, mine, lags, 0, unroll=2)
    sums = jnp.sum(red[...], axis=2)
    sums = jnp.concatenate([sums[:, :order], -res_plain_ref[...] * sums[:, order:]], axis=1)
    red_send[...] = jnp.concatenate([sums, jnp.zeros((mine, LANES - 2 * order), F32)], axis=1)
    r_copies = [
        remote(red_send, red_recv.at[me_d], r_ss.at[i], r_rs.at[i], dp=peer)
        for i, peer in enumerate(dp_peers)
    ]
    for copy in r_copies:
        copy.start()
    red_recv[me_d] = red_send[...]
    for j in range(n_ctx):
        part = slice(j * mine, (j + 1) * mine)
        gk_ref[j] = (gprod[part, :] * qkv_recv[j, 2].astype(F32)).astype(BF16)
        gv_ref[j] = (gprod[part, :] * qkv_recv[j, 1].astype(F32)).astype(BF16)
    for copy in f_copies:
        copy.wait()
    dw_ref[...] = dwf[...]
    for copy in r_copies:
        copy.wait()
    total = red_recv[0]
    for d in range(1, n_dp):
        total = total + red_recv[d]
    par_ref[...] = total


def fused_body(n_dp, n_ctx, queries, keys, values, grad_out, out_weight, residues, decays):
    chans, block = out_weight.shape
    mine, order = residues.shape
    width = block // n_dp
    wide = (mine, order, LANES)
    vm = pl.BlockSpec(memory_space=pltpu.VMEM)
    hbm = pl.BlockSpec(memory_space=pl.ANY)
    sem = pltpu.SemaphoreType.DMA
    n_c, n_d, half = n_ctx - 1, n_dp - 1, n_ctx // 2

    def twice(*shape):
        return [sem(shape), sem(shape)]

    scratch = [
        pltpu.VMEM((3, chans, LANES), BF16),
        pltpu.VMEM((n_ctx, 3, mine, LANES), BF16),
        pltpu.VMEM((n_ctx, n_dp * LANES, width), BF16),
        pltpu.VMEM((n_ctx, chans, width), BF16),
        pltpu.VMEM((mine, LANES, n_ctx * LANES), BF16),
        pltpu.VMEM((mine, 4 * order, n_ctx * LANES), BF16),
        pltpu.VMEM((chans, LANES), F32),
        pltpu.VMEM((chans, LANES), F32),
        pltpu.VMEM((chans, LANES), F32),
        pltpu.VMEM((chans, LANES), F32),
        pltpu.VMEM((n_ctx, mine, LANES), BF16),
        pltpu.VMEM((chans, n_dp * LANES), BF16),
        pltpu.VMEM((chans, n_dp * LANES), F32),
        pltpu.VMEM((chans, n_dp * LANES), BF16),
        pltpu.VMEM((n_dp, chans, LANES), BF16),
        pltpu.VMEM((chans, LANES), BF16),
        pltpu.VMEM((n_ctx, mine, LANES), BF16),
        pltpu.VMEM((n_ctx, chans, width), BF16),
        pltpu.VMEM((half, chans, width), BF16),
        pltpu.VMEM((half - 1, chans, width), BF16),
        pltpu.VMEM((chans, block), BF16),
        pltpu.VMEM((mine, 2 * order, LANES), F32),
        pltpu.VMEM((mine, LANES), F32),
        pltpu.VMEM((n_dp, mine, LANES), F32),
    ]
    scratch += twice(n_c) + twice(n_d, n_ctx) + twice(n_c) + twice(n_c) + twice(n_d) + twice(n_d)
    scratch += twice(n_c) + twice(half) + twice(half - 1) + twice(n_d) + twice(n_d) + [sem((n_ctx + 1,))]
    blocks = jax.ShapeDtypeStruct((n_ctx, mine, LANES), BF16)
    gq, gk, gv, dw, par = pl.pallas_call(
        functools.partial(fused_kernel, n_dp, n_ctx),
        out_shape=(
            blocks, blocks, blocks,
            jax.ShapeDtypeStruct((chans, block), BF16),
            jax.ShapeDtypeStruct((mine, LANES), F32),
        ),
        in_specs=[vm, vm, vm, hbm, hbm, vm, vm, vm],
        out_specs=(vm,) * 5,
        scratch_shapes=scratch,
        compiler_params=pltpu.CompilerParams(
            collective_id=0, has_side_effects=True, vmem_limit_bytes=58 * 1024 * 1024
        ),
        cost_estimate=pl.CostEstimate(flops=6 * 10**9, bytes_accessed=8 * 2**20, transcendentals=2**20),
    )(
        queries, keys, values, grad_out, out_weight,
        jnp.broadcast_to(decays[:, :, None], wide),
        jnp.broadcast_to(residues[:, :, None], wide),
        residues,
    )

    def positions_first(grid):
        return jnp.transpose(grid, (0, 2, 1)).reshape(1, n_ctx * LANES, mine)

    return (
        positions_first(gq), positions_first(gk), positions_first(gv),
        dw.astype(F32), par[:, :order], par[:, order : 2 * order],
    )


def fits_fused(n_dp, n_ctx, queries, grad_out, out_weight, residues):
    chans, columns = out_weight.shape
    return (
        n_ctx == 8
        and n_dp >= 2
        and queries.shape[0] == n_dp
        and queries.shape[1] == n_ctx * LANES
        and chans % (n_ctx * 16) == 0
        and chans % LANES == 0
        and columns % (n_ctx * n_dp * LANES) == 0
        and residues.shape[1] % 16 == 0
        and 2 * residues.shape[1] <= LANES
        and chans <= 512
        and columns <= 8192
    )


def solution(mesh):
    placed = (
        P("dp", "ctx", None),
        P("dp", "ctx", None),
        P("dp", "ctx", None),
        P("dp", "ctx", None),
        P(None, "ctx"),
        P("ctx", None),
        P("ctx", None),
    )
    n_dp, n_ctx = mesh.shape["dp"], mesh.shape["ctx"]

    outputs = (
        P("dp", None, "ctx"),
        P("dp", None, "ctx"),
        P("dp", None, "ctx"),
        P(None, "ctx"),
        P("ctx", None),
        P("ctx", None),
    )

    def run(queries, keys, values, grad_out, out_weight, residues, decays):
        inner = body
        if fits_fused(n_dp, n_ctx, queries, grad_out, out_weight, residues):
            inner = functools.partial(fused_body, n_dp, n_ctx)
        mapped = jax.shard_map(inner, mesh=mesh, in_specs=placed, out_specs=outputs, check_vma=False)
        return mapped(queries, keys, values, grad_out, out_weight, residues, decays)

    return run
```

```python
import functools
import math

import jax
import jax.numpy as jnp
from jax import lax
from jax.experimental import pallas as pl
from jax.experimental.pallas import tpu as pltpu
from jax.sharding import PartitionSpec as P

FFT_COLS = 128


HIGHEST = lax.Precision.HIGHEST


def fourier_tables(fft_rows, fft_cols):
    total = fft_rows * fft_cols
    row_index = jnp.arange(fft_rows, dtype=jnp.int32)
    col_index = jnp.arange(fft_cols, dtype=jnp.int32)
    first = (row_index[:, None] * row_index[None, :] % fft_rows).astype(jnp.float32) * (
        2.0 * math.pi / fft_rows
    )
    twist = (row_index[:, None] * col_index[None, :] % total).astype(jnp.float32) * (
        2.0 * math.pi / total
    )
    second = (col_index[:, None] * col_index[None, :] % fft_cols).astype(jnp.float32) * (
        2.0 * math.pi / fft_cols
    )
    return (
        (jnp.cos(first), -jnp.sin(first)),
        (jnp.cos(twist), -jnp.sin(twist)),
        (jnp.cos(second), -jnp.sin(second)),
    )


def complex_product(left_re, left_im, right_re, right_im):
    return (left_re * right_re - left_im * right_im, left_re * right_im + left_im * right_re)


def apply_middle(table_re, table_im, data_re):

    def single(table, data):
        return jnp.einsum("kn,cnm->ckm", table, data, precision=HIGHEST)

    return (single(table_re, data_re), single(table_im, data_re))


def apply_last(table_re, table_im, data_re, data_im):

    def single(data, table):
        return jnp.einsum("ckm,mj->ckj", data, table, precision=HIGHEST)

    return (
        single(data_re, table_re) - single(data_im, table_im),
        single(data_im, table_re) + single(data_re, table_im),
    )


def forward_transform(signal, tables):
    (first_re, first_im), (twist_re, twist_im), (second_re, second_im) = tables
    section_re, section_im = apply_middle(first_re, first_im, signal)
    section_re, section_im = complex_product(section_re, section_im, twist_re, twist_im)
    return apply_last(second_re, second_im, section_re, section_im)


def inverse_transform(spec_re, spec_im, tables):
    (first_re, first_im), (twist_re, twist_im), (second_re, second_im) = tables
    section_re, section_im = apply_last(second_re, -second_im, spec_re, spec_im)
    section_re, section_im = complex_product(section_re, section_im, twist_re, -twist_im)
    result = jnp.einsum("kn,cnm->ckm", first_re, section_re, precision=HIGHEST) + jnp.einsum(
        "kn,cnm->ckm", first_im, section_im, precision=HIGHEST
    )
    total = first_re.shape[0] * second_re.shape[0]
    return result / float(total)


def padded_grid(signal, fft_rows, fft_cols):
    channels, seq_len = signal.shape
    padded = jnp.concatenate(
        [signal, jnp.zeros((channels, fft_rows * fft_cols - seq_len), jnp.float32)], axis=1
    )
    return padded.reshape(channels, fft_rows, fft_cols)


def leading_part(grid, seq_len):
    return grid.reshape(grid.shape[0], -1)[:, :seq_len]


def channels_first(block):
    return block[0].astype(jnp.float32).T


def rounded_sum(terms):
    rounded = lax.optimization_barrier(terms.astype(jnp.bfloat16))
    return jnp.sum(rounded.astype(jnp.float32), axis=0)


def body(queries, keys, values, grad_out, out_weight, residues, decays):
    channels = out_weight.shape[0]
    block_width = out_weight.shape[1]
    tok_rows = grad_out.shape[1]
    grad_cols = lax.all_to_all(grad_out, "ctx", split_axis=2, concat_axis=1, tiled=True)
    shard_piece = lax.all_gather(out_weight, "ctx", axis=1, tiled=True)
    blocks = shard_piece.shape[1] // block_width
    partial_value = grad_out[0]
    partial_value = partial_value.reshape(tok_rows, blocks, block_width)
    weight_part = shard_piece.reshape(channels, blocks, block_width)
    terms = jnp.einsum(
        "tks,cks->ktc", partial_value, weight_part, preferred_element_type=jnp.float32
    )
    gated_sum = rounded_sum(terms)
    grad_gated = gated_sum.astype(jnp.bfloat16)[None]
    query_ch, key_ch, value_ch, gated_grad_ch = (
        lax.all_to_all(queries, "ctx", split_axis=2, concat_axis=1, tiled=True),
        lax.all_to_all(keys, "ctx", split_axis=2, concat_axis=1, tiled=True),
        lax.all_to_all(values, "ctx", split_axis=2, concat_axis=1, tiled=True),
        lax.all_to_all(grad_gated, "ctx", split_axis=2, concat_axis=1, tiled=True),
    )
    grad_gated_full = channels_first(gated_grad_ch)
    seq_len = query_ch.shape[1]
    fft_rows = 2 * seq_len // FFT_COLS
    tables = fourier_tables(fft_rows, FFT_COLS)
    query_full = channels_first(query_ch)
    key_full = channels_first(key_ch)
    value_full = channels_first(value_ch)
    positions = jnp.arange(seq_len).astype(jnp.float32)
    decay_terms = jnp.exp(-decays[:, :, None] * positions[None, None, :])
    filter_taps = jnp.sum(residues[:, :, None] * decay_terms, axis=1)
    product = key_full * value_full
    grad_conv = grad_gated_full * query_full
    prod_re, prod_im = forward_transform(padded_grid(product, fft_rows, FFT_COLS), tables)
    taps_re, taps_im = forward_transform(padded_grid(filter_taps, fft_rows, FFT_COLS), tables)
    grad_re, grad_im = forward_transform(padded_grid(grad_conv, fft_rows, FFT_COLS), tables)
    conv_out = leading_part(
        inverse_transform(*complex_product(prod_re, prod_im, taps_re, taps_im), tables), seq_len
    )
    grad_product = leading_part(
        inverse_transform(*complex_product(taps_re, -taps_im, grad_re, grad_im), tables), seq_len
    )
    grad_taps = leading_part(
        inverse_transform(*complex_product(prod_re, -prod_im, grad_re, grad_im), tables), seq_len
    )
    gated = (query_full * conv_out).T.astype(jnp.bfloat16)[None]
    grad_queries = (grad_gated_full * conv_out).T.astype(jnp.bfloat16)[None]
    grad_keys = (grad_product * value_full).T.astype(jnp.bfloat16)[None]
    grad_values = (grad_product * key_full).T.astype(jnp.bfloat16)[None]
    partial_value = lax.dot_general(
        lax.all_gather(gated, "ctx", axis=2, tiled=True)[0],
        grad_cols[0],
        (((0,), (0,)), ((), ())),
        preferred_element_type=jnp.float32,
    )
    grad_weight = partial_value
    grad_residues = jnp.sum(grad_taps[:, None, :] * decay_terms, axis=2)
    grad_decays = -residues * jnp.sum(
        (grad_taps * positions[None, :])[:, None, :] * decay_terms, axis=2
    )
    grad_weight, grad_residues, grad_decays = (
        lax.psum(grad_weight.astype(jnp.bfloat16), "dp").astype(jnp.float32),
        lax.psum(grad_residues.astype(jnp.bfloat16), "dp").astype(jnp.float32),
        lax.psum(grad_decays.astype(jnp.bfloat16), "dp").astype(jnp.float32),
    )
    return (grad_queries, grad_keys, grad_values, grad_weight, grad_residues, grad_decays)

LANES = 128
MESH = pl.DeviceIdType.MESH
F32 = jnp.float32
BF16 = jnp.bfloat16


def dot_nt(left, right):
    return lax.dot_general(left, right, (((1,), (1,)), ((), ())), preferred_element_type=F32)


def split_rows(data):
    high = data.astype(BF16)
    low = (data - high.astype(F32)).astype(BF16)
    return jnp.concatenate([high, low], axis=0)


def fused_kernel(
    n_dp, n_ctx,
    q_ref, k_ref, v_ref, go_ref, w_ref, dec_ref, res_ref,
    gq_ref, gk_ref, gv_ref, dw_ref, par_res_ref, par_dec_ref,
    qkv_send, qkv_recv, gcols, wbuf, toep, etab, utab, vtab, cmat, bmat, dec_wide, res_wide,
    prod, conv, gconv, gprod, ubuf, sbuf, vbuf, zbuf,
    gat_send, gat_all, gg_acc, gg_send, gg_recv, ggt_send, ggt_recv,
    dwp, dwy, dwz, dwf, red, red_send, red_recv,
    q_ss, q_rs, g_ss, g_rs, w_ss, w_rs, a_ss, a_rs, b_ss, b_rs, c_ss, c_rs, t_ss, t_rs,
    y_ss, y_rs, z_ss, z_rs, f_ss, f_rs, r_ss, r_rs, loc_sem,
):
    me_d = lax.axis_index("dp")
    me_c = lax.axis_index("ctx")
    chans = q_ref.shape[2]
    mine = chans // n_ctx
    width = gcols.shape[2]
    order = dec_ref.shape[0]
    block_rows = chans // 2
    half = n_ctx // 2
    side = lax.rem(me_c, 2)
    partner = me_c + 1 - 2 * side
    ctx_peers = [lax.rem(me_c + s, n_ctx) for s in range(1, n_ctx)]
    dp_peers = [lax.rem(me_d + s, n_dp) for s in range(1, n_dp)]
    line_peers = [lax.rem(me_c + 2 * s, n_ctx) for s in range(1, half)]

    def remote(src, dst, ss, rs, **to):
        return pltpu.make_async_remote_copy(
            src_ref=src, dst_ref=dst, send_sem=ss, recv_sem=rs, device_id=to, device_id_type=MESH
        )

    def rows(index, size):
        return pl.ds(pl.multiple_of(index * size, size), size)

    barrier = pltpu.get_barrier_semaphore()
    for peer in ctx_peers:
        pl.semaphore_signal(barrier, inc=1, device_id={"ctx": peer}, device_id_type=MESH)
    for peer in dp_peers:
        pl.semaphore_signal(barrier, inc=1, device_id={"dp": peer}, device_id_type=MESH)

    for part, ref in enumerate((q_ref, k_ref, v_ref)):
        for at in range(0, chans, LANES):
            qkv_send[part, at : at + LANES, :] = ref[0, :, at : at + LANES].astype(F32).T.astype(BF16)
    pl.semaphore_wait(barrier, n_ctx - 1 + n_dp - 1)

    q_copies = [
        remote(qkv_send.at[:, rows(peer, mine), :], qkv_recv.at[me_c], q_ss.at[i], q_rs.at[i], ctx=peer)
        for i, peer in enumerate(ctx_peers)
    ]
    for copy in q_copies:
        copy.start()
    qkv_recv[me_c] = qkv_send[:, rows(me_c, mine), :]

    def cols_copy(i, peer, k):
        return remote(
            go_ref.at[0, :, rows(k * n_dp + peer, width)],
            gcols.at[k, rows(me_d, LANES), :],
            g_ss.at[i, k], g_rs.at[i, k], dp=peer,
        )

    def cols_own(k):
        return pltpu.make_async_copy(
            go_ref.at[0, :, rows(k * n_dp + me_d, width)], gcols.at[k, rows(me_d, LANES), :], loc_sem.at[k]
        )

    for k in range(n_ctx):
        for i, peer in enumerate(dp_peers):
            cols_copy(i, peer, k).start()
        cols_own(k).start()

    own_w = pltpu.make_async_copy(w_ref.at[:, rows(me_d, width)], wbuf.at[me_c], loc_sem.at[n_ctx])
    own_w.start()
    w_own = w_ref.at[:, rows(me_d, width)]
    w_copies = [
        remote(w_own, wbuf.at[me_c], w_ss.at[i], w_rs.at[i], ctx=peer)
        for i, peer in enumerate(line_peers + [partner])
    ]
    for copy in w_copies:
        copy.start()

    lane = lax.broadcasted_iota(jnp.int32, (order, LANES), 1).astype(F32)
    upper = lax.broadcasted_iota(jnp.int32, (LANES, LANES), 1) >= lax.broadcasted_iota(
        jnp.int32, (LANES, LANES), 0
    )
    column = lax.broadcasted_iota(jnp.int32, (mine, LANES), 1)
    rates, weights = dec_ref[...], res_ref[...]
    for c in range(mine):
        dec_wide[c] = jnp.broadcast_to(rates[:, c : c + 1], (order, LANES))
        res_wide[c] = jnp.broadcast_to(weights[:, c : c + 1], (order, LANES))
    rate_rows, weight_rows = rates.T, weights.T
    rest = jnp.zeros((mine, LANES - 2 * order), F32)
    fade = jnp.exp(-float(LANES) * jnp.concatenate([rate_rows, rate_rows, rest], axis=1))
    step = jnp.where((column >= order) & (column < 2 * order), float(LANES), 0.0)
    weight_rows = jnp.concatenate([weight_rows, jnp.zeros((mine, LANES - order), F32)], axis=1)
    blank = jnp.zeros((LANES - 2 * order, LANES), F32)

    def tables(c, carry):
        rate = dec_wide[c]
        weight = res_wide[c]
        value = jnp.exp(-rate * lane)
        etab[c] = jnp.concatenate([split_rows(value), split_rows(value * lane)], axis=0)
        after = jnp.exp(-rate * (lane + 1.0))
        before = jnp.exp(-rate * (LANES - 1.0 - lane))
        cmat[c] = (weight * after).astype(BF16)
        bmat[c] = before.astype(BF16)
        vtab[c] = jnp.concatenate([after, after * (lane + 1.0), blank], axis=0).astype(BF16)
        utab[c] = jnp.concatenate([before, before * (LANES - 1.0 - lane), blank], axis=0).astype(BF16)
        taps = jnp.sum(weight * value, axis=0, keepdims=True)
        rolled = pltpu.roll(jnp.broadcast_to(taps, (LANES, LANES)), 0, 1, stride=1, stride_axis=0)
        toep[c] = jnp.where(upper, rolled, 0.0).astype(BF16)
        return carry

    lax.fori_loop(0, mine, tables, 0, unroll=4)

    def channel(ref, c):
        return ref[pl.ds(c, n_ctx, stride=mine), :]

    def joined(both):
        return both[:n_ctx] + both[n_ctx:]

    for copy in q_copies:
        copy.wait()
    for j in range(n_ctx):
        prod[j * mine : (j + 1) * mine, :] = qkv_recv[j, 1].astype(F32) * qkv_recv[j, 2].astype(F32)

    def enter(c, carry):
        ubuf[pl.ds(c, n_ctx, stride=mine), :] = joined(dot_nt(split_rows(channel(prod, c)), utab[c]))
        return carry

    lax.fori_loop(0, mine, enter, 0, unroll=8)
    state = jnp.zeros((mine, LANES), F32)
    for j in range(n_ctx):
        part = slice(j * mine, (j + 1) * mine)
        sbuf[part, :] = state
        state = fade * (state + step * pltpu.roll(state, order, 1)) + ubuf[part, :]

    def forward(c, carry):
        near = jnp.dot(split_rows(channel(prod, c)), toep[c], preferred_element_type=F32)
        far = jnp.dot(split_rows(channel(sbuf, c))[:, :order], cmat[c], preferred_element_type=F32)
        conv[pl.ds(c, n_ctx, stride=mine), :] = joined(near + far)
        return carry

    lax.fori_loop(0, mine, forward, 0, unroll=8)

    for j in range(n_ctx):
        gat_send[j] = (qkv_recv[j, 0].astype(F32) * conv[j * mine : (j + 1) * mine, :]).astype(BF16)
    a_copies = [
        remote(
            gat_send.at[peer],
            gat_all.at[rows(me_c, mine), rows(me_d, LANES)],
            a_ss.at[i], a_rs.at[i], ctx=peer,
        )
        for i, peer in enumerate(ctx_peers)
    ]
    for copy in a_copies:
        copy.start()
    gat_all[rows(me_c, mine), rows(me_d, LANES)] = gat_send[me_c]

    for copy in a_copies:
        copy.wait()
    b_copies = [
        remote(
            gat_all.at[:, rows(me_d, LANES)], gat_all.at[:, rows(me_d, LANES)],
            b_ss.at[i], b_rs.at[i], dp=peer,
        )
        for i, peer in enumerate(dp_peers)
    ]
    for copy in b_copies:
        copy.start()

    forwards = []
    for i, peer in enumerate(line_peers):
        w_copies[i].wait()
        source = lax.rem(me_c + n_ctx - 2 * (i + 1), n_ctx)
        copy = remote(wbuf.at[source], wbuf.at[source], w_ss.at[half + i], w_rs.at[half + i], ctx=partner)
        copy.start()
        forwards.append(copy)

    for copy in b_copies:
        copy.wait()
    for k in range(n_ctx):
        for i, peer in enumerate(dp_peers):
            cols_copy(i, peer, k).wait()
        cols_own(k).wait()

    def weight_block(k, h):
        part = slice(h * block_rows, (h + 1) * block_rows)
        dwp[k, part, :] = jnp.dot(gat_all[part, :], gcols[k], preferred_element_type=F32).astype(BF16)

    def part_of(h):
        return slice(h * block_rows, (h + 1) * block_rows)

    line = me_c // 2
    y_copies = {}
    for h in range(2):
        for s in list(range(1, half)) + [0]:
            k = 2 * lax.rem(line + s, half) + 1 - side
            weight_block(k, h)
            copy = remote(
                dwp.at[k, part_of(h), :], dwy.at[s, part_of(h), :], y_ss.at[h, s], y_rs.at[h, s], ctx=partner
            )
            copy.start()
            y_copies[h, s] = copy

    def own_blocks(z, carry):
        for h in range(2):
            weight_block(2 * z + side, h)
        return carry

    lax.fori_loop(0, half, own_blocks, 0)

    own_w.wait()
    w_copies[half - 1].wait()
    for copy in forwards:
        copy.wait()
    gg_acc[...] = jnp.zeros_like(gg_acc)

    def terms(k, carry):
        gg_acc[...] += dot_nt(wbuf[k], gcols[k])
        return carry

    z_copies = {}

    def pass_on(h):
        part = part_of(h)
        for i, peer in enumerate(line_peers):
            y_copies[h, i + 1].wait()
            dwp[peer, part, :] = (dwp[peer, part, :].astype(F32) + dwy[i + 1, part, :].astype(F32)).astype(BF16)
            copy = remote(
                dwp.at[peer, part, :], dwz.at[i, part, :], z_ss.at[h, i], z_rs.at[h, i], ctx=peer
            )
            copy.start()
            z_copies[h, i] = copy

    def finish(h):
        part = part_of(h)
        for i in range(half - 1):
            z_copies[h, i].wait()
        y_copies[h, 0].wait()
        last = dwp[me_c, part, :].astype(F32) + dwy[0, part, :].astype(F32)
        for i in range(half - 1):
            last = last + dwz[i, part, :].astype(F32)
        dwf[part, rows(me_d, width)] = last.astype(BF16)
        copies = [
            remote(
                dwf.at[part, rows(me_d, width)], dwf.at[part, rows(me_d, width)],
                f_ss.at[h, i], f_rs.at[h, i], dp=peer,
            )
            for i, peer in enumerate(dp_peers)
        ]
        for copy in copies:
            copy.start()
        return copies

    lax.fori_loop(0, n_ctx, terms, 0)
    gg_send[...] = gg_acc[...].astype(BF16)
    c_copies = [
        remote(gg_send.at[:, rows(peer, LANES)], gg_recv.at[me_d], c_ss.at[i], c_rs.at[i], dp=peer)
        for i, peer in enumerate(dp_peers)
    ]
    for copy in c_copies:
        copy.start()
    gg_recv[me_d] = gg_send[:, rows(me_d, LANES)]
    pass_on(0)

    for copy in c_copies:
        copy.wait()
    total = gg_recv[0].astype(F32)
    for d in range(1, n_dp):
        total = total + gg_recv[d].astype(F32)
    ggt_send[...] = total.astype(BF16)
    t_copies = [
        remote(ggt_send.at[rows(peer, mine), :], ggt_recv.at[me_c], t_ss.at[i], t_rs.at[i], ctx=peer)
        for i, peer in enumerate(ctx_peers)
    ]
    for copy in t_copies:
        copy.start()
    ggt_recv[me_c] = ggt_send[rows(me_c, mine), :]
    pass_on(1)

    for copy in t_copies:
        copy.wait()
    for j in range(n_ctx):
        part = slice(j * mine, (j + 1) * mine)
        gated_grad = ggt_recv[j].astype(F32)
        gconv[part, :] = gated_grad * qkv_recv[j, 0].astype(F32)
        gq_ref[:, j * LANES : (j + 1) * LANES] = (gated_grad * conv[part, :]).astype(BF16)

    def leave(c, carry):
        vbuf[pl.ds(c, n_ctx, stride=mine), :] = joined(dot_nt(split_rows(channel(gconv, c)), vtab[c]))
        return carry

    lax.fori_loop(0, mine, leave, 0, unroll=8)
    state = jnp.zeros((mine, LANES), F32)
    plain_sum, timed_sum = state, state
    for j in reversed(range(n_ctx)):
        part = slice(j * mine, (j + 1) * mine)
        zbuf[part, :] = state
        left, right = vbuf[part, :], sbuf[part, :]
        state = fade * state + weight_rows * left
        plain_sum = plain_sum + left * right
        timed_sum = timed_sum + left * pltpu.roll(right, order, 1) + pltpu.roll(left, order, 1) * right
    far_sums = jnp.where(column < order, plain_sum, jnp.where(column < 2 * order, timed_sum, 0.0))

    def backward(c, carry):
        near = dot_nt(split_rows(channel(gconv, c)), toep[c])
        far = jnp.dot(split_rows(channel(zbuf, c))[:, :order], bmat[c], preferred_element_type=F32)
        gprod[pl.ds(c, n_ctx, stride=mine), :] = joined(near + far)
        return carry

    def lags(c, carry):
        outer = lax.dot_general(
            channel(prod, c).astype(BF16), channel(gconv, c).astype(BF16),
            (((0,), (0,)), ((), ())), preferred_element_type=F32,
        )
        sums = dot_nt(etab[c], jnp.where(upper, outer, 0.0).astype(BF16))
        plain = sums[0:order] + sums[order : 2 * order]
        timed = sums[2 * order : 3 * order] + sums[3 * order :]
        grown = jnp.exp(dec_wide[c] * lane)
        red[c, 0:order, :] = plain * grown
        red[c, order:, :] = (timed - lane * plain) * grown
        return carry

    lax.fori_loop(0, mine, lags, 0, unroll=4)
    f_copies = finish(0)
    sums = jnp.sum(red[...], axis=2)
    sums = jnp.concatenate([sums, rest], axis=1) + far_sums
    red_send[...] = jnp.where(column < order, sums, -pltpu.roll(weight_rows, order, 1) * sums)
    r_copies = [
        remote(red_send, red_recv.at[me_d], r_ss.at[i], r_rs.at[i], dp=peer)
        for i, peer in enumerate(dp_peers)
    ]
    for copy in r_copies:
        copy.start()
    red_recv[me_d] = red_send[...]
    lax.fori_loop(0, mine, backward, 0, unroll=8)
    f_copies += finish(1)
    for j in range(n_ctx):
        part = slice(j * mine, (j + 1) * mine)
        at = slice(j * LANES, (j + 1) * LANES)
        gk_ref[:, at] = (gprod[part, :] * qkv_recv[j, 2].astype(F32)).astype(BF16)
        gv_ref[:, at] = (gprod[part, :] * qkv_recv[j, 1].astype(F32)).astype(BF16)
    for copy in r_copies:
        copy.wait()
    total = red_recv[0]
    for d in range(1, n_dp):
        total = total + red_recv[d]
    turned = total.T
    par_res_ref[...] = turned[0:order, :]
    par_dec_ref[...] = turned[order : 2 * order, :]
    for copy in f_copies:
        copy.wait()
    dw_ref[...] = dwf[...]


def fused_body(n_dp, n_ctx, queries, keys, values, grad_out, out_weight, residues, decays):
    chans, block = out_weight.shape
    mine, order = residues.shape
    width = block // n_dp
    vm = pl.BlockSpec(memory_space=pltpu.VMEM)
    hbm = pl.BlockSpec(memory_space=pl.ANY)
    sem = pltpu.SemaphoreType.DMA
    n_c, n_d, half = n_ctx - 1, n_dp - 1, n_ctx // 2

    def twice(*shape):
        return [sem(shape), sem(shape)]

    scratch = [
        pltpu.VMEM((3, chans, LANES), BF16),
        pltpu.VMEM((n_ctx, 3, mine, LANES), BF16),
        pltpu.VMEM((n_ctx, n_dp * LANES, width), BF16),
        pltpu.VMEM((n_ctx, chans, width), BF16),
        pltpu.VMEM((mine, LANES, LANES), BF16),
        pltpu.VMEM((mine, 4 * order, LANES), BF16),
        pltpu.VMEM((mine, LANES, LANES), BF16),
        pltpu.VMEM((mine, LANES, LANES), BF16),
        pltpu.VMEM((mine, order, LANES), BF16),
        pltpu.VMEM((mine, order, LANES), BF16),
        pltpu.VMEM((mine, order, LANES), F32),
        pltpu.VMEM((mine, order, LANES), F32),
        pltpu.VMEM((chans, LANES), F32),
        pltpu.VMEM((chans, LANES), F32),
        pltpu.VMEM((chans, LANES), F32),
        pltpu.VMEM((chans, LANES), F32),
        pltpu.VMEM((chans, LANES), F32),
        pltpu.VMEM((chans, LANES), F32),
        pltpu.VMEM((chans, LANES), F32),
        pltpu.VMEM((chans, LANES), F32),
        pltpu.VMEM((n_ctx, mine, LANES), BF16),
        pltpu.VMEM((chans, n_dp * LANES), BF16),
        pltpu.VMEM((chans, n_dp * LANES), F32),
        pltpu.VMEM((chans, n_dp * LANES), BF16),
        pltpu.VMEM((n_dp, chans, LANES), BF16),
        pltpu.VMEM((chans, LANES), BF16),
        pltpu.VMEM((n_ctx, mine, LANES), BF16),
        pltpu.VMEM((n_ctx, chans, width), BF16),
        pltpu.VMEM((half, chans, width), BF16),
        pltpu.VMEM((half - 1, chans, width), BF16),
        pltpu.VMEM((chans, block), BF16),
        pltpu.VMEM((mine, 2 * order, LANES), F32),
        pltpu.VMEM((mine, LANES), F32),
        pltpu.VMEM((n_dp, mine, LANES), F32),
    ]
    scratch += twice(n_c) + twice(n_d, n_ctx) + twice(n_c) + twice(n_c) + twice(n_d) + twice(n_d)
    scratch += twice(n_c) + twice(2, half) + twice(2, half - 1) + twice(2, n_d) + twice(n_d) + [sem((n_ctx + 1,))]
    blocks = jax.ShapeDtypeStruct((mine, n_ctx * LANES), BF16)
    params = jax.ShapeDtypeStruct((order, mine), F32)
    gq, gk, gv, dw, par_res, par_dec = pl.pallas_call(
        functools.partial(fused_kernel, n_dp, n_ctx),
        out_shape=(
            blocks, blocks, blocks,
            jax.ShapeDtypeStruct((chans, block), BF16),
            params, params,
        ),
        in_specs=[vm, vm, vm, hbm, hbm, vm, vm],
        out_specs=(vm,) * 6,
        scratch_shapes=scratch,
        compiler_params=pltpu.CompilerParams(
            collective_id=0, has_side_effects=True, vmem_limit_bytes=58 * 1024 * 1024
        ),
        cost_estimate=pl.CostEstimate(flops=6 * 10**9, bytes_accessed=8 * 2**20, transcendentals=2**20),
    )(
        queries, keys, values, grad_out, out_weight,
        decays.T, residues.T,
    )

    def positions_first(grid):
        return grid.T[None]

    return (
        positions_first(gq), positions_first(gk), positions_first(gv),
        dw.astype(F32), par_res.T, par_dec.T,
    )


def fits_fused(n_dp, n_ctx, queries, grad_out, out_weight, residues):
    chans, columns = out_weight.shape
    return (
        n_ctx == 8
        and n_dp >= 2
        and queries.shape[0] == n_dp
        and queries.shape[1] == n_ctx * LANES
        and chans % (n_ctx * 16) == 0
        and chans % LANES == 0
        and columns % (n_ctx * n_dp * LANES) == 0
        and residues.shape[1] % 16 == 0
        and 2 * residues.shape[1] <= LANES
        and chans <= 512
        and columns <= 8192
    )


def solution(mesh):
    placed = (
        P("dp", "ctx", None),
        P("dp", "ctx", None),
        P("dp", "ctx", None),
        P("dp", "ctx", None),
        P(None, "ctx"),
        P("ctx", None),
        P("ctx", None),
    )
    n_dp, n_ctx = mesh.shape["dp"], mesh.shape["ctx"]

    outputs = (
        P("dp", None, "ctx"),
        P("dp", None, "ctx"),
        P("dp", None, "ctx"),
        P(None, "ctx"),
        P("ctx", None),
        P("ctx", None),
    )

    def run(queries, keys, values, grad_out, out_weight, residues, decays):
        inner = body
        if fits_fused(n_dp, n_ctx, queries, grad_out, out_weight, residues):
            inner = functools.partial(fused_body, n_dp, n_ctx)
        mapped = jax.shard_map(inner, mesh=mesh, in_specs=placed, out_specs=outputs, check_vma=False)
        return mapped(queries, keys, values, grad_out, out_weight, residues, decays)

    return run
```

```python
import functools
import math

import jax
import jax.numpy as jnp
from jax import lax
from jax.experimental import pallas as pl
from jax.experimental.pallas import tpu as pltpu
from jax.sharding import PartitionSpec as P

FFT_COLS = 128


HIGHEST = lax.Precision.HIGHEST


def fourier_tables(fft_rows, fft_cols):
    total = fft_rows * fft_cols
    row_index = jnp.arange(fft_rows, dtype=jnp.int32)
    col_index = jnp.arange(fft_cols, dtype=jnp.int32)
    first = (row_index[:, None] * row_index[None, :] % fft_rows).astype(jnp.float32) * (
        2.0 * math.pi / fft_rows
    )
    twist = (row_index[:, None] * col_index[None, :] % total).astype(jnp.float32) * (
        2.0 * math.pi / total
    )
    second = (col_index[:, None] * col_index[None, :] % fft_cols).astype(jnp.float32) * (
        2.0 * math.pi / fft_cols
    )
    return (
        (jnp.cos(first), -jnp.sin(first)),
        (jnp.cos(twist), -jnp.sin(twist)),
        (jnp.cos(second), -jnp.sin(second)),
    )


def complex_product(left_re, left_im, right_re, right_im):
    return (left_re * right_re - left_im * right_im, left_re * right_im + left_im * right_re)


def apply_middle(table_re, table_im, data_re):

    def single(table, data):
        return jnp.einsum("kn,cnm->ckm", table, data, precision=HIGHEST)

    return (single(table_re, data_re), single(table_im, data_re))


def apply_last(table_re, table_im, data_re, data_im):

    def single(data, table):
        return jnp.einsum("ckm,mj->ckj", data, table, precision=HIGHEST)

    return (
        single(data_re, table_re) - single(data_im, table_im),
        single(data_im, table_re) + single(data_re, table_im),
    )


def forward_transform(signal, tables):
    (first_re, first_im), (twist_re, twist_im), (second_re, second_im) = tables
    section_re, section_im = apply_middle(first_re, first_im, signal)
    section_re, section_im = complex_product(section_re, section_im, twist_re, twist_im)
    return apply_last(second_re, second_im, section_re, section_im)


def inverse_transform(spec_re, spec_im, tables):
    (first_re, first_im), (twist_re, twist_im), (second_re, second_im) = tables
    section_re, section_im = apply_last(second_re, -second_im, spec_re, spec_im)
    section_re, section_im = complex_product(section_re, section_im, twist_re, -twist_im)
    result = jnp.einsum("kn,cnm->ckm", first_re, section_re, precision=HIGHEST) + jnp.einsum(
        "kn,cnm->ckm", first_im, section_im, precision=HIGHEST
    )
    total = first_re.shape[0] * second_re.shape[0]
    return result / float(total)


def padded_grid(signal, fft_rows, fft_cols):
    channels, seq_len = signal.shape
    padded = jnp.concatenate(
        [signal, jnp.zeros((channels, fft_rows * fft_cols - seq_len), jnp.float32)], axis=1
    )
    return padded.reshape(channels, fft_rows, fft_cols)


def leading_part(grid, seq_len):
    return grid.reshape(grid.shape[0], -1)[:, :seq_len]


def channels_first(block):
    return block[0].astype(jnp.float32).T


def rounded_sum(terms):
    rounded = lax.optimization_barrier(terms.astype(jnp.bfloat16))
    return jnp.sum(rounded.astype(jnp.float32), axis=0)


def body(queries, keys, values, grad_out, out_weight, residues, decays):
    channels = out_weight.shape[0]
    block_width = out_weight.shape[1]
    tok_rows = grad_out.shape[1]
    grad_cols = lax.all_to_all(grad_out, "ctx", split_axis=2, concat_axis=1, tiled=True)
    shard_piece = lax.all_gather(out_weight, "ctx", axis=1, tiled=True)
    blocks = shard_piece.shape[1] // block_width
    partial_value = grad_out[0]
    partial_value = partial_value.reshape(tok_rows, blocks, block_width)
    weight_part = shard_piece.reshape(channels, blocks, block_width)
    terms = jnp.einsum(
        "tks,cks->ktc", partial_value, weight_part, preferred_element_type=jnp.float32
    )
    gated_sum = rounded_sum(terms)
    grad_gated = gated_sum.astype(jnp.bfloat16)[None]
    query_ch, key_ch, value_ch, gated_grad_ch = (
        lax.all_to_all(queries, "ctx", split_axis=2, concat_axis=1, tiled=True),
        lax.all_to_all(keys, "ctx", split_axis=2, concat_axis=1, tiled=True),
        lax.all_to_all(values, "ctx", split_axis=2, concat_axis=1, tiled=True),
        lax.all_to_all(grad_gated, "ctx", split_axis=2, concat_axis=1, tiled=True),
    )
    grad_gated_full = channels_first(gated_grad_ch)
    seq_len = query_ch.shape[1]
    fft_rows = 2 * seq_len // FFT_COLS
    tables = fourier_tables(fft_rows, FFT_COLS)
    query_full = channels_first(query_ch)
    key_full = channels_first(key_ch)
    value_full = channels_first(value_ch)
    positions = jnp.arange(seq_len).astype(jnp.float32)
    decay_terms = jnp.exp(-decays[:, :, None] * positions[None, None, :])
    filter_taps = jnp.sum(residues[:, :, None] * decay_terms, axis=1)
    product = key_full * value_full
    grad_conv = grad_gated_full * query_full
    prod_re, prod_im = forward_transform(padded_grid(product, fft_rows, FFT_COLS), tables)
    taps_re, taps_im = forward_transform(padded_grid(filter_taps, fft_rows, FFT_COLS), tables)
    grad_re, grad_im = forward_transform(padded_grid(grad_conv, fft_rows, FFT_COLS), tables)
    conv_out = leading_part(
        inverse_transform(*complex_product(prod_re, prod_im, taps_re, taps_im), tables), seq_len
    )
    grad_product = leading_part(
        inverse_transform(*complex_product(taps_re, -taps_im, grad_re, grad_im), tables), seq_len
    )
    grad_taps = leading_part(
        inverse_transform(*complex_product(prod_re, -prod_im, grad_re, grad_im), tables), seq_len
    )
    gated = (query_full * conv_out).T.astype(jnp.bfloat16)[None]
    grad_queries = (grad_gated_full * conv_out).T.astype(jnp.bfloat16)[None]
    grad_keys = (grad_product * value_full).T.astype(jnp.bfloat16)[None]
    grad_values = (grad_product * key_full).T.astype(jnp.bfloat16)[None]
    partial_value = lax.dot_general(
        lax.all_gather(gated, "ctx", axis=2, tiled=True)[0],
        grad_cols[0],
        (((0,), (0,)), ((), ())),
        preferred_element_type=jnp.float32,
    )
    grad_weight = partial_value
    grad_residues = jnp.sum(grad_taps[:, None, :] * decay_terms, axis=2)
    grad_decays = -residues * jnp.sum(
        (grad_taps * positions[None, :])[:, None, :] * decay_terms, axis=2
    )
    grad_weight, grad_residues, grad_decays = (
        lax.psum(grad_weight.astype(jnp.bfloat16), "dp").astype(jnp.float32),
        lax.psum(grad_residues.astype(jnp.bfloat16), "dp").astype(jnp.float32),
        lax.psum(grad_decays.astype(jnp.bfloat16), "dp").astype(jnp.float32),
    )
    return (grad_queries, grad_keys, grad_values, grad_weight, grad_residues, grad_decays)

LANES = 128
PARTS = 4
MESH = pl.DeviceIdType.MESH
F32 = jnp.float32
BF16 = jnp.bfloat16


def dot_nt(left, right):
    return lax.dot_general(left, right, (((1,), (1,)), ((), ())), preferred_element_type=F32)


def split_rows(data):
    high = data.astype(BF16)
    low = (data - high.astype(F32)).astype(BF16)
    return jnp.concatenate([high, low], axis=0)


def fused_kernel(
    n_dp, n_ctx,
    q_ref, k_ref, v_ref, go_ref, w_ref, dec_ref, res_ref,
    gq_ref, gk_ref, gv_ref, dw_ref, par_res_ref, par_dec_ref,
    qkv_send, qkv_recv, gcols, wbuf, toep, etab, utab, vtab, cmat, bmat, dec_wide, res_wide,
    prod, conv, gconv, gprod, ubuf, sbuf, vbuf, zbuf,
    gat_send, gat_all, gg_acc, gg_send, gg_recv, ggt_send, ggt_recv,
    dwp, dwy, dwz, dwf, red, red_send, red_recv,
    q_ss, q_rs, g_ss, g_rs, w_ss, w_rs, a_ss, a_rs, b_ss, b_rs, c_ss, c_rs, t_ss, t_rs,
    y_ss, y_rs, z_ss, z_rs, f_ss, f_rs, r_ss, r_rs, loc_sem,
):
    me_d = lax.axis_index("dp")
    me_c = lax.axis_index("ctx")
    chans = q_ref.shape[2]
    mine = chans // n_ctx
    width = gcols.shape[2]
    order = dec_ref.shape[0]
    block_rows = chans // PARTS
    half = n_ctx // 2
    side = lax.rem(me_c, 2)
    partner = me_c + 1 - 2 * side
    ctx_peers = [lax.rem(me_c + s, n_ctx) for s in range(1, n_ctx)]
    dp_peers = [lax.rem(me_d + s, n_dp) for s in range(1, n_dp)]
    line_peers = [lax.rem(me_c + 2 * s, n_ctx) for s in range(1, half)]

    def remote(src, dst, ss, rs, **to):
        return pltpu.make_async_remote_copy(
            src_ref=src, dst_ref=dst, send_sem=ss, recv_sem=rs, device_id=to, device_id_type=MESH
        )

    def rows(index, size):
        return pl.ds(pl.multiple_of(index * size, size), size)

    barrier = pltpu.get_barrier_semaphore()
    for peer in ctx_peers:
        pl.semaphore_signal(barrier, inc=1, device_id={"ctx": peer}, device_id_type=MESH)
    for peer in dp_peers:
        pl.semaphore_signal(barrier, inc=1, device_id={"dp": peer}, device_id_type=MESH)

    for part, ref in enumerate((q_ref, k_ref, v_ref)):
        for at in range(0, chans, LANES):
            qkv_send[part, at : at + LANES, :] = ref[0, :, at : at + LANES].astype(F32).T.astype(BF16)
    pl.semaphore_wait(barrier, n_ctx - 1 + n_dp - 1)

    q_copies = [
        remote(qkv_send.at[:, rows(peer, mine), :], qkv_recv.at[me_c], q_ss.at[i], q_rs.at[i], ctx=peer)
        for i, peer in enumerate(ctx_peers)
    ]
    for copy in q_copies:
        copy.start()
    qkv_recv[me_c] = qkv_send[:, rows(me_c, mine), :]

    def cols_copy(i, peer, k):
        return remote(
            go_ref.at[0, :, rows(k * n_dp + peer, width)],
            gcols.at[k, rows(me_d, LANES), :],
            g_ss.at[i, k], g_rs.at[i, k], dp=peer,
        )

    def cols_own(k):
        return pltpu.make_async_copy(
            go_ref.at[0, :, rows(k * n_dp + me_d, width)], gcols.at[k, rows(me_d, LANES), :], loc_sem.at[k]
        )

    for k in range(n_ctx):
        for i, peer in enumerate(dp_peers):
            cols_copy(i, peer, k).start()
        cols_own(k).start()

    own_w = pltpu.make_async_copy(w_ref.at[:, rows(me_d, width)], wbuf.at[me_c], loc_sem.at[n_ctx])
    own_w.start()
    w_own = w_ref.at[:, rows(me_d, width)]
    w_copies = [
        remote(w_own, wbuf.at[me_c], w_ss.at[i], w_rs.at[i], ctx=peer)
        for i, peer in enumerate(line_peers + [partner])
    ]
    w_copies[half - 1].start()

    lane = lax.broadcasted_iota(jnp.int32, (order, LANES), 1).astype(F32)
    upper = lax.broadcasted_iota(jnp.int32, (LANES, LANES), 1) >= lax.broadcasted_iota(
        jnp.int32, (LANES, LANES), 0
    )
    column = lax.broadcasted_iota(jnp.int32, (mine, LANES), 1)
    rates, weights = dec_ref[...], res_ref[...]
    for c in range(mine):
        dec_wide[c] = jnp.broadcast_to(rates[:, c : c + 1], (order, LANES))
        res_wide[c] = jnp.broadcast_to(weights[:, c : c + 1], (order, LANES))
    rate_rows, weight_rows = rates.T, weights.T
    rest = jnp.zeros((mine, LANES - 2 * order), F32)
    fade = jnp.exp(-float(LANES) * jnp.concatenate([rate_rows, rate_rows, rest], axis=1))
    step = jnp.where((column >= order) & (column < 2 * order), float(LANES), 0.0)
    weight_rows = jnp.concatenate([weight_rows, jnp.zeros((mine, LANES - order), F32)], axis=1)
    blank = jnp.zeros((LANES - 2 * order, LANES), F32)

    def tables(c, carry):
        rate = dec_wide[c]
        weight = res_wide[c]
        value = jnp.exp(-rate * lane)
        etab[c] = jnp.concatenate([split_rows(value), split_rows(value * lane)], axis=0)
        after = jnp.exp(-rate * (lane + 1.0))
        before = jnp.exp(-rate * (LANES - 1.0 - lane))
        cmat[c] = (weight * after).astype(BF16)
        bmat[c] = before.astype(BF16)
        vtab[c] = jnp.concatenate([after, after * (lane + 1.0), blank], axis=0).astype(BF16)
        utab[c] = jnp.concatenate([before, before * (LANES - 1.0 - lane), blank], axis=0).astype(BF16)
        taps = jnp.sum(weight * value, axis=0, keepdims=True)
        rolled = pltpu.roll(jnp.broadcast_to(taps, (LANES, LANES)), 0, 1, stride=1, stride_axis=0)
        toep[c] = jnp.where(upper, rolled, 0.0).astype(BF16)
        return carry

    lax.fori_loop(0, mine, tables, 0, unroll=4)

    def channel(ref, c):
        return ref[pl.ds(c, n_ctx, stride=mine), :]

    def joined(both):
        return both[:n_ctx] + both[n_ctx:]

    for copy in q_copies:
        copy.wait()
    for copy in w_copies[: half - 1]:
        copy.start()
    for j in range(n_ctx):
        prod[j * mine : (j + 1) * mine, :] = qkv_recv[j, 1].astype(F32) * qkv_recv[j, 2].astype(F32)

    def enter(c, carry):
        ubuf[pl.ds(c, n_ctx, stride=mine), :] = joined(dot_nt(split_rows(channel(prod, c)), utab[c]))
        return carry

    lax.fori_loop(0, mine, enter, 0, unroll=8)
    state = jnp.zeros((mine, LANES), F32)
    for j in range(n_ctx):
        part = slice(j * mine, (j + 1) * mine)
        sbuf[part, :] = state
        state = fade * (state + step * pltpu.roll(state, order, 1)) + ubuf[part, :]

    def forward(c, carry):
        near = jnp.dot(split_rows(channel(prod, c)), toep[c], preferred_element_type=F32)
        far = jnp.dot(split_rows(channel(sbuf, c))[:, :order], cmat[c], preferred_element_type=F32)
        conv[pl.ds(c, n_ctx, stride=mine), :] = joined(near + far)
        return carry

    lax.fori_loop(0, mine, forward, 0, unroll=8)

    for j in range(n_ctx):
        gat_send[j] = (qkv_recv[j, 0].astype(F32) * conv[j * mine : (j + 1) * mine, :]).astype(BF16)
    a_copies = [
        remote(
            gat_send.at[peer],
            gat_all.at[rows(me_c, mine), rows(me_d, LANES)],
            a_ss.at[i], a_rs.at[i], ctx=peer,
        )
        for i, peer in enumerate(ctx_peers)
    ]
    for copy in a_copies:
        copy.start()
    gat_all[rows(me_c, mine), rows(me_d, LANES)] = gat_send[me_c]

    for copy in a_copies:
        copy.wait()
    b_copies = [
        remote(
            gat_all.at[:, rows(me_d, LANES)], gat_all.at[:, rows(me_d, LANES)],
            b_ss.at[i], b_rs.at[i], dp=peer,
        )
        for i, peer in enumerate(dp_peers)
    ]
    for copy in b_copies:
        copy.start()

    forwards = []

    def forward_weights(i):
        w_copies[i].wait()
        source = lax.rem(me_c + n_ctx - 2 * (i + 1), n_ctx)
        copy = remote(wbuf.at[source], wbuf.at[source], w_ss.at[half + i], w_rs.at[half + i], ctx=partner)
        copy.start()
        forwards.append(copy)

    forward_weights(0)
    for copy in b_copies:
        copy.wait()
    for k in range(n_ctx):
        for i, peer in enumerate(dp_peers):
            cols_copy(i, peer, k).wait()
        cols_own(k).wait()

    def weight_block(k, h):
        part = slice(h * block_rows, (h + 1) * block_rows)
        dwp[k, part, :] = jnp.dot(gat_all[part, :], gcols[k], preferred_element_type=F32).astype(BF16)

    def part_of(h):
        return slice(h * block_rows, (h + 1) * block_rows)

    line = me_c // 2
    y_copies = {}
    for h in range(PARTS):
        for s in list(range(1, half)) + [0]:
            k = 2 * lax.rem(line + s, half) + 1 - side
            weight_block(k, h)
            copy = remote(
                dwp.at[k, part_of(h), :], dwy.at[s, part_of(h), :], y_ss.at[h, s], y_rs.at[h, s], ctx=partner
            )
            copy.start()
            y_copies[h, s] = copy
        if h + 1 < half - 1:
            forward_weights(h + 1)

    def own_blocks(z, carry):
        for h in range(PARTS):
            weight_block(2 * z + side, h)
        return carry

    lax.fori_loop(0, half, own_blocks, 0)

    z_copies = {}

    def pass_on(h):
        part = part_of(h)
        for i, peer in enumerate(line_peers):
            y_copies[h, i + 1].wait()
            dwp[peer, part, :] = (dwp[peer, part, :].astype(F32) + dwy[i + 1, part, :].astype(F32)).astype(BF16)
            copy = remote(
                dwp.at[peer, part, :], dwz.at[i, part, :], z_ss.at[h, i], z_rs.at[h, i], ctx=peer
            )
            copy.start()
            z_copies[h, i] = copy

    def finish(h):
        part = part_of(h)
        for i in range(half - 1):
            z_copies[h, i].wait()
        y_copies[h, 0].wait()
        last = dwp[me_c, part, :].astype(F32) + dwy[0, part, :].astype(F32)
        for i in range(half - 1):
            last = last + dwz[i, part, :].astype(F32)
        dwf[part, rows(me_d, width)] = last.astype(BF16)
        copies = [
            remote(
                dwf.at[part, rows(me_d, width)], dwf.at[part, rows(me_d, width)],
                f_ss.at[h, i], f_rs.at[h, i], dp=peer,
            )
            for i, peer in enumerate(dp_peers)
        ]
        for copy in copies:
            copy.start()
        return copies

    pass_on(0)
    own_w.wait()
    w_copies[half - 1].wait()
    for copy in forwards:
        copy.wait()
    gg_acc[...] = jnp.zeros_like(gg_acc)

    def terms(k, carry):
        gg_acc[...] += dot_nt(wbuf[k], gcols[k])
        return carry

    lax.fori_loop(0, n_ctx, terms, 0)
    gg_send[...] = gg_acc[...].astype(BF16)
    c_copies = [
        remote(gg_send.at[:, rows(peer, LANES)], gg_recv.at[me_d], c_ss.at[i], c_rs.at[i], dp=peer)
        for i, peer in enumerate(dp_peers)
    ]
    for copy in c_copies:
        copy.start()
    gg_recv[me_d] = gg_send[:, rows(me_d, LANES)]
    pass_on(1)

    for copy in c_copies:
        copy.wait()
    total = gg_recv[0].astype(F32)
    for d in range(1, n_dp):
        total = total + gg_recv[d].astype(F32)
    ggt_send[...] = total.astype(BF16)
    t_copies = [
        remote(ggt_send.at[rows(peer, mine), :], ggt_recv.at[me_c], t_ss.at[i], t_rs.at[i], ctx=peer)
        for i, peer in enumerate(ctx_peers)
    ]
    for copy in t_copies:
        copy.start()
    ggt_recv[me_c] = ggt_send[rows(me_c, mine), :]
    pass_on(2)
    f_copies = finish(0)
    pass_on(3)

    for copy in t_copies:
        copy.wait()
    for j in range(n_ctx):
        part = slice(j * mine, (j + 1) * mine)
        gated_grad = ggt_recv[j].astype(F32)
        gconv[part, :] = gated_grad * qkv_recv[j, 0].astype(F32)
        gq_ref[:, j * LANES : (j + 1) * LANES] = (gated_grad * conv[part, :]).astype(BF16)

    def leave(c, carry):
        vbuf[pl.ds(c, n_ctx, stride=mine), :] = joined(dot_nt(split_rows(channel(gconv, c)), vtab[c]))
        return carry

    lax.fori_loop(0, mine, leave, 0, unroll=8)
    state = jnp.zeros((mine, LANES), F32)
    plain_sum, timed_sum = state, state
    for j in reversed(range(n_ctx)):
        part = slice(j * mine, (j + 1) * mine)
        zbuf[part, :] = state
        left, right = vbuf[part, :], sbuf[part, :]
        state = fade * state + weight_rows * left
        plain_sum = plain_sum + left * right
        timed_sum = timed_sum + left * pltpu.roll(right, order, 1) + pltpu.roll(left, order, 1) * right
    far_sums = jnp.where(column < order, plain_sum, jnp.where(column < 2 * order, timed_sum, 0.0))

    def backward(c, carry):
        near = dot_nt(split_rows(channel(gconv, c)), toep[c])
        far = jnp.dot(split_rows(channel(zbuf, c))[:, :order], bmat[c], preferred_element_type=F32)
        gprod[pl.ds(c, n_ctx, stride=mine), :] = joined(near + far)
        return carry

    def lags(c, carry):
        outer = lax.dot_general(
            channel(prod, c).astype(BF16), channel(gconv, c).astype(BF16),
            (((0,), (0,)), ((), ())), preferred_element_type=F32,
        )
        sums = dot_nt(etab[c], jnp.where(upper, outer, 0.0).astype(BF16))
        plain = sums[0:order] + sums[order : 2 * order]
        timed = sums[2 * order : 3 * order] + sums[3 * order :]
        grown = jnp.exp(dec_wide[c] * lane)
        red[c, 0:order, :] = plain * grown
        red[c, order:, :] = (timed - lane * plain) * grown
        return carry

    f_copies += finish(1)
    lax.fori_loop(0, mine, lags, 0, unroll=4)
    f_copies += finish(2)
    sums = jnp.sum(red[...], axis=2)
    sums = jnp.concatenate([sums, rest], axis=1) + far_sums
    red_send[...] = jnp.where(column < order, sums, -pltpu.roll(weight_rows, order, 1) * sums)
    r_copies = [
        remote(red_send, red_recv.at[me_d], r_ss.at[i], r_rs.at[i], dp=peer)
        for i, peer in enumerate(dp_peers)
    ]
    for copy in r_copies:
        copy.start()
    red_recv[me_d] = red_send[...]
    lax.fori_loop(0, mine, backward, 0, unroll=8)
    f_copies += finish(3)
    for j in range(n_ctx):
        part = slice(j * mine, (j + 1) * mine)
        at = slice(j * LANES, (j + 1) * LANES)
        gk_ref[:, at] = (gprod[part, :] * qkv_recv[j, 2].astype(F32)).astype(BF16)
        gv_ref[:, at] = (gprod[part, :] * qkv_recv[j, 1].astype(F32)).astype(BF16)
    for copy in r_copies:
        copy.wait()
    total = red_recv[0]
    for d in range(1, n_dp):
        total = total + red_recv[d]
    turned = total.T
    par_res_ref[...] = turned[0:order, :]
    par_dec_ref[...] = turned[order : 2 * order, :]
    for copy in f_copies:
        copy.wait()
    dw_ref[...] = dwf[...]


def fused_body(n_dp, n_ctx, queries, keys, values, grad_out, out_weight, residues, decays):
    chans, block = out_weight.shape
    mine, order = residues.shape
    width = block // n_dp
    vm = pl.BlockSpec(memory_space=pltpu.VMEM)
    hbm = pl.BlockSpec(memory_space=pl.ANY)
    sem = pltpu.SemaphoreType.DMA
    n_c, n_d, half = n_ctx - 1, n_dp - 1, n_ctx // 2

    def twice(*shape):
        return [sem(shape), sem(shape)]

    scratch = [
        pltpu.VMEM((3, chans, LANES), BF16),
        pltpu.VMEM((n_ctx, 3, mine, LANES), BF16),
        pltpu.VMEM((n_ctx, n_dp * LANES, width), BF16),
        pltpu.VMEM((n_ctx, chans, width), BF16),
        pltpu.VMEM((mine, LANES, LANES), BF16),
        pltpu.VMEM((mine, 4 * order, LANES), BF16),
        pltpu.VMEM((mine, LANES, LANES), BF16),
        pltpu.VMEM((mine, LANES, LANES), BF16),
        pltpu.VMEM((mine, order, LANES), BF16),
        pltpu.VMEM((mine, order, LANES), BF16),
        pltpu.VMEM((mine, order, LANES), F32),
        pltpu.VMEM((mine, order, LANES), F32),
        pltpu.VMEM((chans, LANES), F32),
        pltpu.VMEM((chans, LANES), F32),
        pltpu.VMEM((chans, LANES), F32),
        pltpu.VMEM((chans, LANES), F32),
        pltpu.VMEM((chans, LANES), F32),
        pltpu.VMEM((chans, LANES), F32),
        pltpu.VMEM((chans, LANES), F32),
        pltpu.VMEM((chans, LANES), F32),
        pltpu.VMEM((n_ctx, mine, LANES), BF16),
        pltpu.VMEM((chans, n_dp * LANES), BF16),
        pltpu.VMEM((chans, n_dp * LANES), F32),
        pltpu.VMEM((chans, n_dp * LANES), BF16),
        pltpu.VMEM((n_dp, chans, LANES), BF16),
        pltpu.VMEM((chans, LANES), BF16),
        pltpu.VMEM((n_ctx, mine, LANES), BF16),
        pltpu.VMEM((n_ctx, chans, width), BF16),
        pltpu.VMEM((half, chans, width), BF16),
        pltpu.VMEM((half - 1, chans, width), BF16),
        pltpu.VMEM((chans, block), BF16),
        pltpu.VMEM((mine, 2 * order, LANES), F32),
        pltpu.VMEM((mine, LANES), F32),
        pltpu.VMEM((n_dp, mine, LANES), F32),
    ]
    scratch += twice(n_c) + twice(n_d, n_ctx) + twice(n_c) + twice(n_c) + twice(n_d) + twice(n_d)
    scratch += twice(n_c) + twice(PARTS, half) + twice(PARTS, half - 1) + twice(PARTS, n_d) + twice(n_d) + [sem((n_ctx + 1,))]
    blocks = jax.ShapeDtypeStruct((mine, n_ctx * LANES), BF16)
    params = jax.ShapeDtypeStruct((order, mine), F32)
    gq, gk, gv, dw, par_res, par_dec = pl.pallas_call(
        functools.partial(fused_kernel, n_dp, n_ctx),
        out_shape=(
            blocks, blocks, blocks,
            jax.ShapeDtypeStruct((chans, block), BF16),
            params, params,
        ),
        in_specs=[vm, vm, vm, hbm, hbm, vm, vm],
        out_specs=(vm,) * 6,
        scratch_shapes=scratch,
        compiler_params=pltpu.CompilerParams(
            collective_id=0, has_side_effects=True, vmem_limit_bytes=58 * 1024 * 1024
        ),
        cost_estimate=pl.CostEstimate(flops=6 * 10**9, bytes_accessed=8 * 2**20, transcendentals=2**20),
    )(
        queries, keys, values, grad_out, out_weight,
        decays.T, residues.T,
    )

    def positions_first(grid):
        return grid.T[None]

    return (
        positions_first(gq), positions_first(gk), positions_first(gv),
        dw.astype(F32), par_res.T, par_dec.T,
    )


def fits_fused(n_dp, n_ctx, queries, grad_out, out_weight, residues):
    chans, columns = out_weight.shape
    return (
        n_ctx == 8
        and n_dp >= 2
        and queries.shape[0] == n_dp
        and queries.shape[1] == n_ctx * LANES
        and chans % (n_ctx * 16) == 0
        and chans % LANES == 0
        and columns % (n_ctx * n_dp * LANES) == 0
        and residues.shape[1] % 16 == 0
        and 2 * residues.shape[1] <= LANES
        and chans <= 512
        and columns <= 8192
    )


def solution(mesh):
    placed = (
        P("dp", "ctx", None),
        P("dp", "ctx", None),
        P("dp", "ctx", None),
        P("dp", "ctx", None),
        P(None, "ctx"),
        P("ctx", None),
        P("ctx", None),
    )
    n_dp, n_ctx = mesh.shape["dp"], mesh.shape["ctx"]

    outputs = (
        P("dp", None, "ctx"),
        P("dp", None, "ctx"),
        P("dp", None, "ctx"),
        P(None, "ctx"),
        P("ctx", None),
        P("ctx", None),
    )

    def run(queries, keys, values, grad_out, out_weight, residues, decays):
        inner = body
        if fits_fused(n_dp, n_ctx, queries, grad_out, out_weight, residues):
            inner = functools.partial(fused_body, n_dp, n_ctx)
        mapped = jax.shard_map(inner, mesh=mesh, in_specs=placed, out_specs=outputs, check_vma=False)
        return mapped(queries, keys, values, grad_out, out_weight, residues, decays)

    return run
```

```python
import functools
import math

import jax
import jax.numpy as jnp
from jax import lax
from jax.experimental import pallas as pl
from jax.experimental.pallas import tpu as pltpu
from jax.sharding import PartitionSpec as P

FFT_COLS = 128


HIGHEST = lax.Precision.HIGHEST


def fourier_tables(fft_rows, fft_cols):
    total = fft_rows * fft_cols
    row_index = jnp.arange(fft_rows, dtype=jnp.int32)
    col_index = jnp.arange(fft_cols, dtype=jnp.int32)
    first = (row_index[:, None] * row_index[None, :] % fft_rows).astype(jnp.float32) * (
        2.0 * math.pi / fft_rows
    )
    twist = (row_index[:, None] * col_index[None, :] % total).astype(jnp.float32) * (
        2.0 * math.pi / total
    )
    second = (col_index[:, None] * col_index[None, :] % fft_cols).astype(jnp.float32) * (
        2.0 * math.pi / fft_cols
    )
    return (
        (jnp.cos(first), -jnp.sin(first)),
        (jnp.cos(twist), -jnp.sin(twist)),
        (jnp.cos(second), -jnp.sin(second)),
    )


def complex_product(left_re, left_im, right_re, right_im):
    return (left_re * right_re - left_im * right_im, left_re * right_im + left_im * right_re)


def apply_middle(table_re, table_im, data_re):

    def single(table, data):
        return jnp.einsum("kn,cnm->ckm", table, data, precision=HIGHEST)

    return (single(table_re, data_re), single(table_im, data_re))


def apply_last(table_re, table_im, data_re, data_im):

    def single(data, table):
        return jnp.einsum("ckm,mj->ckj", data, table, precision=HIGHEST)

    return (
        single(data_re, table_re) - single(data_im, table_im),
        single(data_im, table_re) + single(data_re, table_im),
    )


def forward_transform(signal, tables):
    (first_re, first_im), (twist_re, twist_im), (second_re, second_im) = tables
    section_re, section_im = apply_middle(first_re, first_im, signal)
    section_re, section_im = complex_product(section_re, section_im, twist_re, twist_im)
    return apply_last(second_re, second_im, section_re, section_im)


def inverse_transform(spec_re, spec_im, tables):
    (first_re, first_im), (twist_re, twist_im), (second_re, second_im) = tables
    section_re, section_im = apply_last(second_re, -second_im, spec_re, spec_im)
    section_re, section_im = complex_product(section_re, section_im, twist_re, -twist_im)
    result = jnp.einsum("kn,cnm->ckm", first_re, section_re, precision=HIGHEST) + jnp.einsum(
        "kn,cnm->ckm", first_im, section_im, precision=HIGHEST
    )
    total = first_re.shape[0] * second_re.shape[0]
    return result / float(total)


def padded_grid(signal, fft_rows, fft_cols):
    channels, seq_len = signal.shape
    padded = jnp.concatenate(
        [signal, jnp.zeros((channels, fft_rows * fft_cols - seq_len), jnp.float32)], axis=1
    )
    return padded.reshape(channels, fft_rows, fft_cols)


def leading_part(grid, seq_len):
    return grid.reshape(grid.shape[0], -1)[:, :seq_len]


def channels_first(block):
    return block[0].astype(jnp.float32).T


def rounded_sum(terms):
    rounded = lax.optimization_barrier(terms.astype(jnp.bfloat16))
    return jnp.sum(rounded.astype(jnp.float32), axis=0)


def body(queries, keys, values, grad_out, out_weight, residues, decays):
    channels = out_weight.shape[0]
    block_width = out_weight.shape[1]
    tok_rows = grad_out.shape[1]
    grad_cols = lax.all_to_all(grad_out, "ctx", split_axis=2, concat_axis=1, tiled=True)
    shard_piece = lax.all_gather(out_weight, "ctx", axis=1, tiled=True)
    blocks = shard_piece.shape[1] // block_width
    partial_value = grad_out[0]
    partial_value = partial_value.reshape(tok_rows, blocks, block_width)
    weight_part = shard_piece.reshape(channels, blocks, block_width)
    terms = jnp.einsum(
        "tks,cks->ktc", partial_value, weight_part, preferred_element_type=jnp.float32
    )
    gated_sum = rounded_sum(terms)
    grad_gated = gated_sum.astype(jnp.bfloat16)[None]
    query_ch, key_ch, value_ch, gated_grad_ch = (
        lax.all_to_all(queries, "ctx", split_axis=2, concat_axis=1, tiled=True),
        lax.all_to_all(keys, "ctx", split_axis=2, concat_axis=1, tiled=True),
        lax.all_to_all(values, "ctx", split_axis=2, concat_axis=1, tiled=True),
        lax.all_to_all(grad_gated, "ctx", split_axis=2, concat_axis=1, tiled=True),
    )
    grad_gated_full = channels_first(gated_grad_ch)
    seq_len = query_ch.shape[1]
    fft_rows = 2 * seq_len // FFT_COLS
    tables = fourier_tables(fft_rows, FFT_COLS)
    query_full = channels_first(query_ch)
    key_full = channels_first(key_ch)
    value_full = channels_first(value_ch)
    positions = jnp.arange(seq_len).astype(jnp.float32)
    decay_terms = jnp.exp(-decays[:, :, None] * positions[None, None, :])
    filter_taps = jnp.sum(residues[:, :, None] * decay_terms, axis=1)
    product = key_full * value_full
    grad_conv = grad_gated_full * query_full
    prod_re, prod_im = forward_transform(padded_grid(product, fft_rows, FFT_COLS), tables)
    taps_re, taps_im = forward_transform(padded_grid(filter_taps, fft_rows, FFT_COLS), tables)
    grad_re, grad_im = forward_transform(padded_grid(grad_conv, fft_rows, FFT_COLS), tables)
    conv_out = leading_part(
        inverse_transform(*complex_product(prod_re, prod_im, taps_re, taps_im), tables), seq_len
    )
    grad_product = leading_part(
        inverse_transform(*complex_product(taps_re, -taps_im, grad_re, grad_im), tables), seq_len
    )
    grad_taps = leading_part(
        inverse_transform(*complex_product(prod_re, -prod_im, grad_re, grad_im), tables), seq_len
    )
    gated = (query_full * conv_out).T.astype(jnp.bfloat16)[None]
    grad_queries = (grad_gated_full * conv_out).T.astype(jnp.bfloat16)[None]
    grad_keys = (grad_product * value_full).T.astype(jnp.bfloat16)[None]
    grad_values = (grad_product * key_full).T.astype(jnp.bfloat16)[None]
    partial_value = lax.dot_general(
        lax.all_gather(gated, "ctx", axis=2, tiled=True)[0],
        grad_cols[0],
        (((0,), (0,)), ((), ())),
        preferred_element_type=jnp.float32,
    )
    grad_weight = partial_value
    grad_residues = jnp.sum(grad_taps[:, None, :] * decay_terms, axis=2)
    grad_decays = -residues * jnp.sum(
        (grad_taps * positions[None, :])[:, None, :] * decay_terms, axis=2
    )
    grad_weight, grad_residues, grad_decays = (
        lax.psum(grad_weight.astype(jnp.bfloat16), "dp").astype(jnp.float32),
        lax.psum(grad_residues.astype(jnp.bfloat16), "dp").astype(jnp.float32),
        lax.psum(grad_decays.astype(jnp.bfloat16), "dp").astype(jnp.float32),
    )
    return (grad_queries, grad_keys, grad_values, grad_weight, grad_residues, grad_decays)

LANES = 128
PARTS = 4
MESH = pl.DeviceIdType.MESH
F32 = jnp.float32
BF16 = jnp.bfloat16


def dot_nt(left, right):
    return lax.dot_general(left, right, (((1,), (1,)), ((), ())), preferred_element_type=F32)


def split_rows(data):
    high = data.astype(BF16)
    low = (data - high.astype(F32)).astype(BF16)
    return jnp.concatenate([high, low], axis=0)


def fused_kernel(
    n_dp, n_ctx,
    q_ref, k_ref, v_ref, go_ref, w_ref, dec_ref, res_ref,
    gq_ref, gk_ref, gv_ref, dw_ref, par_res_ref, par_dec_ref,
    qkv_send, qkv_recv, gcols, wbuf, toep, etab, utab, vtab, cmat, bmat, dec_wide, res_wide,
    prod, conv, gconv, gprod, ubuf, sbuf, vbuf, zbuf,
    gat_send, gat_all, gg_acc, gg_send, gg_recv, ggt_send, ggt_recv,
    dwp, dwy, dwz, dwf, red, red_send, red_recv,
    q_ss, q_rs, g_ss, g_rs, w_ss, w_rs, a_ss, a_rs, b_ss, b_rs, c_ss, c_rs, t_ss, t_rs,
    y_ss, y_rs, z_ss, z_rs, f_ss, f_rs, r_ss, r_rs, loc_sem,
):
    me_d = lax.axis_index("dp")
    me_c = lax.axis_index("ctx")
    chans = q_ref.shape[2]
    mine = chans // n_ctx
    width = gcols.shape[2]
    order = dec_ref.shape[0]
    block_rows = chans // PARTS
    half = n_ctx // 2
    side = lax.rem(me_c, 2)
    partner = me_c + 1 - 2 * side
    ctx_peers = [lax.rem(me_c + s, n_ctx) for s in range(1, n_ctx)]
    dp_peers = [lax.rem(me_d + s, n_dp) for s in range(1, n_dp)]
    sibling = me_d + 1 - 2 * lax.rem(me_d, 2)
    far_peers = [lax.rem(me_d + 2 * s, n_dp) for s in range(1, n_dp // 2)]
    far_sources = [lax.rem(me_d + n_dp - 2 * s, n_dp) for s in range(1, n_dp // 2)]
    line_peers = [lax.rem(me_c + 2 * s, n_ctx) for s in range(1, half)]

    def remote(src, dst, ss, rs, **to):
        return pltpu.make_async_remote_copy(
            src_ref=src, dst_ref=dst, send_sem=ss, recv_sem=rs, device_id=to, device_id_type=MESH
        )

    def rows(index, size):
        return pl.ds(pl.multiple_of(index * size, size), size)

    barrier = pltpu.get_barrier_semaphore()
    for peer in ctx_peers:
        pl.semaphore_signal(barrier, inc=1, device_id={"ctx": peer}, device_id_type=MESH)
    for peer in dp_peers:
        pl.semaphore_signal(barrier, inc=1, device_id={"dp": peer}, device_id_type=MESH)

    for part, ref in enumerate((q_ref, k_ref, v_ref)):
        for at in range(0, chans, LANES):
            qkv_send[part, at : at + LANES, :] = ref[0, :, at : at + LANES].astype(F32).T.astype(BF16)
    pl.semaphore_wait(barrier, n_ctx - 1 + n_dp - 1)

    q_copies = [
        remote(qkv_send.at[:, rows(peer, mine), :], qkv_recv.at[me_c], q_ss.at[i], q_rs.at[i], ctx=peer)
        for i, peer in enumerate(ctx_peers)
    ]
    for copy in q_copies:
        copy.start()
    qkv_recv[me_c] = qkv_send[:, rows(me_c, mine), :]

    def cols_copy(i, peer, k):
        return remote(
            go_ref.at[0, :, rows(k * n_dp + peer, width)],
            gcols.at[k, rows(me_d, LANES), :],
            g_ss.at[i, k], g_rs.at[i, k], dp=peer,
        )

    def cols_own(k):
        return pltpu.make_async_copy(
            go_ref.at[0, :, rows(k * n_dp + me_d, width)], gcols.at[k, rows(me_d, LANES), :], loc_sem.at[k]
        )

    for k in range(n_ctx):
        for i, peer in enumerate(dp_peers):
            cols_copy(i, peer, k).start()
        cols_own(k).start()

    own_w = pltpu.make_async_copy(w_ref.at[:, rows(me_d, width)], wbuf.at[me_c], loc_sem.at[n_ctx])
    own_w.start()
    w_own = w_ref.at[:, rows(me_d, width)]
    w_copies = [
        remote(w_own, wbuf.at[me_c], w_ss.at[i], w_rs.at[i], ctx=peer)
        for i, peer in enumerate(line_peers + [partner])
    ]
    w_copies[half - 1].start()

    lane = lax.broadcasted_iota(jnp.int32, (order, LANES), 1).astype(F32)
    upper = lax.broadcasted_iota(jnp.int32, (LANES, LANES), 1) >= lax.broadcasted_iota(
        jnp.int32, (LANES, LANES), 0
    )
    column = lax.broadcasted_iota(jnp.int32, (mine, LANES), 1)
    rates, weights = dec_ref[...], res_ref[...]
    for c in range(mine):
        dec_wide[c] = jnp.broadcast_to(rates[:, c : c + 1], (order, LANES))
        res_wide[c] = jnp.broadcast_to(weights[:, c : c + 1], (order, LANES))
    rate_rows, weight_rows = rates.T, weights.T
    rest = jnp.zeros((mine, LANES - 2 * order), F32)
    fade = jnp.exp(-float(LANES) * jnp.concatenate([rate_rows, rate_rows, rest], axis=1))
    step = jnp.where((column >= order) & (column < 2 * order), float(LANES), 0.0)
    weight_rows = jnp.concatenate([weight_rows, jnp.zeros((mine, LANES - order), F32)], axis=1)
    blank = jnp.zeros((LANES - 2 * order, LANES), F32)

    def tables(c, carry):
        rate = dec_wide[c]
        weight = res_wide[c]
        value = jnp.exp(-rate * lane)
        etab[c] = jnp.concatenate([split_rows(value), split_rows(value * lane)], axis=0)
        after = jnp.exp(-rate * (lane + 1.0))
        before = jnp.exp(-rate * (LANES - 1.0 - lane))
        cmat[c] = (weight * after).astype(BF16)
        bmat[c] = before.astype(BF16)
        vtab[c] = jnp.concatenate([after, after * (lane + 1.0), blank], axis=0).astype(BF16)
        utab[c] = jnp.concatenate([before, before * (LANES - 1.0 - lane), blank], axis=0).astype(BF16)
        taps = jnp.sum(weight * value, axis=0, keepdims=True)
        rolled = pltpu.roll(jnp.broadcast_to(taps, (LANES, LANES)), 0, 1, stride=1, stride_axis=0)
        toep[c] = jnp.where(upper, rolled, 0.0).astype(BF16)
        return carry

    lax.fori_loop(0, mine, tables, 0, unroll=4)

    def channel(ref, c):
        return ref[pl.ds(c, n_ctx, stride=mine), :]

    def joined(both):
        return both[:n_ctx] + both[n_ctx:]

    for copy in q_copies:
        copy.wait()
    for copy in w_copies[: half - 1]:
        copy.start()
    w_copies[half - 1].wait()
    for i, peer in enumerate(line_peers):
        copy = remote(
            wbuf.at[partner], wbuf.at[partner], w_ss.at[half + i], w_rs.at[half + i], ctx=peer
        )
        copy.start()
        w_copies.append(copy)
    for j in range(n_ctx):
        prod[j * mine : (j + 1) * mine, :] = qkv_recv[j, 1].astype(F32) * qkv_recv[j, 2].astype(F32)

    def enter(c, carry):
        ubuf[pl.ds(c, n_ctx, stride=mine), :] = joined(dot_nt(split_rows(channel(prod, c)), utab[c]))
        return carry

    lax.fori_loop(0, mine, enter, 0, unroll=8)
    state = jnp.zeros((mine, LANES), F32)
    for j in range(n_ctx):
        part = slice(j * mine, (j + 1) * mine)
        sbuf[part, :] = state
        state = fade * (state + step * pltpu.roll(state, order, 1)) + ubuf[part, :]

    def forward(c, carry):
        near = jnp.dot(split_rows(channel(prod, c)), toep[c], preferred_element_type=F32)
        far = jnp.dot(split_rows(channel(sbuf, c))[:, :order], cmat[c], preferred_element_type=F32)
        conv[pl.ds(c, n_ctx, stride=mine), :] = joined(near + far)
        return carry

    lax.fori_loop(0, mine, forward, 0, unroll=8)

    for j in range(n_ctx):
        gat_send[j] = (qkv_recv[j, 0].astype(F32) * conv[j * mine : (j + 1) * mine, :]).astype(BF16)
    a_copies = [
        remote(
            gat_send.at[peer],
            gat_all.at[rows(me_c, mine), rows(me_d, LANES)],
            a_ss.at[i], a_rs.at[i], ctx=peer,
        )
        for i, peer in enumerate(ctx_peers)
    ]
    for copy in a_copies:
        copy.start()
    gat_all[rows(me_c, mine), rows(me_d, LANES)] = gat_send[me_c]

    for copy in a_copies:
        copy.wait()
    b_copies = [
        remote(
            gat_all.at[:, rows(me_d, LANES)], gat_all.at[:, rows(me_d, LANES)],
            b_ss.at[i], b_rs.at[i], dp=peer,
        )
        for i, peer in enumerate(far_peers + [sibling])
    ]
    for copy in b_copies:
        copy.start()

    for i, source in enumerate(far_sources):
        b_copies[i].wait()
        copy = remote(
            gat_all.at[:, rows(source, LANES)], gat_all.at[:, rows(source, LANES)],
            b_ss.at[n_dp // 2 + i], b_rs.at[n_dp // 2 + i], dp=sibling,
        )
        copy.start()
        b_copies.append(copy)
    for copy in b_copies[n_dp // 2 - 1 :]:
        copy.wait()
    for k in range(n_ctx):
        for i, peer in enumerate(dp_peers):
            cols_copy(i, peer, k).wait()
        cols_own(k).wait()

    def weight_block(k, h):
        part = slice(h * block_rows, (h + 1) * block_rows)
        dwp[k, part, :] = jnp.dot(gat_all[part, :], gcols[k], preferred_element_type=F32).astype(BF16)

    def part_of(h):
        return slice(h * block_rows, (h + 1) * block_rows)

    line = me_c // 2
    y_copies = {}
    for h in range(PARTS):
        for s in list(range(1, half)) + [0]:
            k = 2 * lax.rem(line + s, half) + 1 - side
            weight_block(k, h)
            copy = remote(
                dwp.at[k, part_of(h), :], dwy.at[s, part_of(h), :], y_ss.at[h, s], y_rs.at[h, s], ctx=partner
            )
            copy.start()
            y_copies[h, s] = copy

    def own_blocks(z, carry):
        for h in range(PARTS):
            weight_block(2 * z + side, h)
        return carry

    lax.fori_loop(0, half, own_blocks, 0)

    z_copies = {}

    def pass_on(h):
        part = part_of(h)
        for i, peer in enumerate(line_peers):
            y_copies[h, i + 1].wait()
            dwp[peer, part, :] = (dwp[peer, part, :].astype(F32) + dwy[i + 1, part, :].astype(F32)).astype(BF16)
            copy = remote(
                dwp.at[peer, part, :], dwz.at[i, part, :], z_ss.at[h, i], z_rs.at[h, i], ctx=peer
            )
            copy.start()
            z_copies[h, i] = copy

    def finish(h):
        part = part_of(h)
        for i in range(half - 1):
            z_copies[h, i].wait()
        y_copies[h, 0].wait()
        last = dwp[me_c, part, :].astype(F32) + dwy[0, part, :].astype(F32)
        for i in range(half - 1):
            last = last + dwz[i, part, :].astype(F32)
        dwf[part, rows(me_d, width)] = last.astype(BF16)
        copies = [
            remote(
                dwf.at[part, rows(me_d, width)], dwf.at[part, rows(me_d, width)],
                f_ss.at[h, i], f_rs.at[h, i], dp=peer,
            )
            for i, peer in enumerate(far_peers + [sibling])
        ]
        for copy in copies:
            copy.start()
        return copies

    def share(h):
        part = part_of(h)
        for i, source in enumerate(far_sources):
            f_copies[h][i].wait()
            copy = remote(
                dwf.at[part, rows(source, width)], dwf.at[part, rows(source, width)],
                f_ss.at[h, n_dp // 2 + i], f_rs.at[h, n_dp // 2 + i], dp=sibling,
            )
            copy.start()
            f_copies[h].append(copy)

    pass_on(0)
    own_w.wait()
    for copy in w_copies[: half - 1] + w_copies[half:]:
        copy.wait()
    gg_acc[...] = jnp.zeros_like(gg_acc)

    def terms(k, carry):
        gg_acc[...] += dot_nt(wbuf[k], gcols[k])
        return carry

    lax.fori_loop(0, n_ctx, terms, 0)
    gg_send[...] = gg_acc[...].astype(BF16)
    c_copies = [
        remote(gg_send.at[:, rows(peer, LANES)], gg_recv.at[me_d], c_ss.at[i], c_rs.at[i], dp=peer)
        for i, peer in enumerate(dp_peers)
    ]
    for copy in c_copies:
        copy.start()
    gg_recv[me_d] = gg_send[:, rows(me_d, LANES)]
    pass_on(1)

    for copy in c_copies:
        copy.wait()
    total = gg_recv[0].astype(F32)
    for d in range(1, n_dp):
        total = total + gg_recv[d].astype(F32)
    ggt_send[...] = total.astype(BF16)
    t_copies = [
        remote(ggt_send.at[rows(peer, mine), :], ggt_recv.at[me_c], t_ss.at[i], t_rs.at[i], ctx=peer)
        for i, peer in enumerate(ctx_peers)
    ]
    for copy in t_copies:
        copy.start()
    ggt_recv[me_c] = ggt_send[rows(me_c, mine), :]
    pass_on(2)
    f_copies = [finish(0)]
    pass_on(3)

    for copy in t_copies:
        copy.wait()
    for j in range(n_ctx):
        part = slice(j * mine, (j + 1) * mine)
        gated_grad = ggt_recv[j].astype(F32)
        gconv[part, :] = gated_grad * qkv_recv[j, 0].astype(F32)
        gq_ref[:, j * LANES : (j + 1) * LANES] = (gated_grad * conv[part, :]).astype(BF16)

    def leave(c, carry):
        vbuf[pl.ds(c, n_ctx, stride=mine), :] = joined(dot_nt(split_rows(channel(gconv, c)), vtab[c]))
        return carry

    lax.fori_loop(0, mine, leave, 0, unroll=8)
    state = jnp.zeros((mine, LANES), F32)
    plain_sum, timed_sum = state, state
    for j in reversed(range(n_ctx)):
        part = slice(j * mine, (j + 1) * mine)
        zbuf[part, :] = state
        left, right = vbuf[part, :], sbuf[part, :]
        state = fade * state + weight_rows * left
        plain_sum = plain_sum + left * right
        timed_sum = timed_sum + left * pltpu.roll(right, order, 1) + pltpu.roll(left, order, 1) * right
    far_sums = jnp.where(column < order, plain_sum, jnp.where(column < 2 * order, timed_sum, 0.0))

    def backward(c, carry):
        near = dot_nt(split_rows(channel(gconv, c)), toep[c])
        far = jnp.dot(split_rows(channel(zbuf, c))[:, :order], bmat[c], preferred_element_type=F32)
        gprod[pl.ds(c, n_ctx, stride=mine), :] = joined(near + far)
        return carry

    def lags(c, carry):
        outer = lax.dot_general(
            channel(prod, c).astype(BF16), channel(gconv, c).astype(BF16),
            (((0,), (0,)), ((), ())), preferred_element_type=F32,
        )
        sums = dot_nt(etab[c], jnp.where(upper, outer, 0.0).astype(BF16))
        plain = sums[0:order] + sums[order : 2 * order]
        timed = sums[2 * order : 3 * order] + sums[3 * order :]
        grown = jnp.exp(dec_wide[c] * lane)
        red[c, 0:order, :] = plain * grown
        red[c, order:, :] = (timed - lane * plain) * grown
        return carry

    f_copies.append(finish(1))
    share(0)
    lax.fori_loop(0, mine, lags, 0, unroll=4)
    f_copies.append(finish(2))
    share(1)
    sums = jnp.sum(red[...], axis=2)
    sums = jnp.concatenate([sums, rest], axis=1) + far_sums
    red_send[...] = jnp.where(column < order, sums, -pltpu.roll(weight_rows, order, 1) * sums)
    r_copies = [
        remote(red_send, red_recv.at[me_d], r_ss.at[i], r_rs.at[i], dp=peer)
        for i, peer in enumerate(dp_peers)
    ]
    for copy in r_copies:
        copy.start()
    red_recv[me_d] = red_send[...]
    lax.fori_loop(0, mine, backward, 0, unroll=8)
    f_copies.append(finish(3))
    share(2)
    for j in range(n_ctx):
        part = slice(j * mine, (j + 1) * mine)
        at = slice(j * LANES, (j + 1) * LANES)
        gk_ref[:, at] = (gprod[part, :] * qkv_recv[j, 2].astype(F32)).astype(BF16)
        gv_ref[:, at] = (gprod[part, :] * qkv_recv[j, 1].astype(F32)).astype(BF16)
    share(3)
    for copy in r_copies:
        copy.wait()
    total = red_recv[0]
    for d in range(1, n_dp):
        total = total + red_recv[d]
    turned = total.T
    par_res_ref[...] = turned[0:order, :]
    par_dec_ref[...] = turned[order : 2 * order, :]
    for copies in f_copies:
        for copy in copies[n_dp // 2 - 1 :]:
            copy.wait()
    dw_ref[...] = dwf[...]


def fused_body(n_dp, n_ctx, queries, keys, values, grad_out, out_weight, residues, decays):
    chans, block = out_weight.shape
    mine, order = residues.shape
    width = block // n_dp
    vm = pl.BlockSpec(memory_space=pltpu.VMEM)
    hbm = pl.BlockSpec(memory_space=pl.ANY)
    sem = pltpu.SemaphoreType.DMA
    n_c, n_d, half = n_ctx - 1, n_dp - 1, n_ctx // 2

    def twice(*shape):
        return [sem(shape), sem(shape)]

    scratch = [
        pltpu.VMEM((3, chans, LANES), BF16),
        pltpu.VMEM((n_ctx, 3, mine, LANES), BF16),
        pltpu.VMEM((n_ctx, n_dp * LANES, width), BF16),
        pltpu.VMEM((n_ctx, chans, width), BF16),
        pltpu.VMEM((mine, LANES, LANES), BF16),
        pltpu.VMEM((mine, 4 * order, LANES), BF16),
        pltpu.VMEM((mine, LANES, LANES), BF16),
        pltpu.VMEM((mine, LANES, LANES), BF16),
        pltpu.VMEM((mine, order, LANES), BF16),
        pltpu.VMEM((mine, order, LANES), BF16),
        pltpu.VMEM((mine, order, LANES), F32),
        pltpu.VMEM((mine, order, LANES), F32),
        pltpu.VMEM((chans, LANES), F32),
        pltpu.VMEM((chans, LANES), F32),
        pltpu.VMEM((chans, LANES), F32),
        pltpu.VMEM((chans, LANES), F32),
        pltpu.VMEM((chans, LANES), F32),
        pltpu.VMEM((chans, LANES), F32),
        pltpu.VMEM((chans, LANES), F32),
        pltpu.VMEM((chans, LANES), F32),
        pltpu.VMEM((n_ctx, mine, LANES), BF16),
        pltpu.VMEM((chans, n_dp * LANES), BF16),
        pltpu.VMEM((chans, n_dp * LANES), F32),
        pltpu.VMEM((chans, n_dp * LANES), BF16),
        pltpu.VMEM((n_dp, chans, LANES), BF16),
        pltpu.VMEM((chans, LANES), BF16),
        pltpu.VMEM((n_ctx, mine, LANES), BF16),
        pltpu.VMEM((n_ctx, chans, width), BF16),
        pltpu.VMEM((half, chans, width), BF16),
        pltpu.VMEM((half - 1, chans, width), BF16),
        pltpu.VMEM((chans, block), BF16),
        pltpu.VMEM((mine, 2 * order, LANES), F32),
        pltpu.VMEM((mine, LANES), F32),
        pltpu.VMEM((n_dp, mine, LANES), F32),
    ]
    scratch += twice(n_c) + twice(n_d, n_ctx) + twice(n_c) + twice(n_c) + twice(n_d) + twice(n_d)
    scratch += twice(n_c) + twice(PARTS, half) + twice(PARTS, half - 1) + twice(PARTS, n_d) + twice(n_d) + [sem((n_ctx + 1,))]
    blocks = jax.ShapeDtypeStruct((mine, n_ctx * LANES), BF16)
    params = jax.ShapeDtypeStruct((order, mine), F32)
    gq, gk, gv, dw, par_res, par_dec = pl.pallas_call(
        functools.partial(fused_kernel, n_dp, n_ctx),
        out_shape=(
            blocks, blocks, blocks,
            jax.ShapeDtypeStruct((chans, block), BF16),
            params, params,
        ),
        in_specs=[vm, vm, vm, hbm, hbm, vm, vm],
        out_specs=(vm,) * 6,
        scratch_shapes=scratch,
        compiler_params=pltpu.CompilerParams(
            collective_id=0, has_side_effects=True, vmem_limit_bytes=58 * 1024 * 1024
        ),
        cost_estimate=pl.CostEstimate(flops=6 * 10**9, bytes_accessed=8 * 2**20, transcendentals=2**20),
    )(
        queries, keys, values, grad_out, out_weight,
        decays.T, residues.T,
    )

    def positions_first(grid):
        return grid.T[None]

    return (
        positions_first(gq), positions_first(gk), positions_first(gv),
        dw.astype(F32), par_res.T, par_dec.T,
    )


def fits_fused(n_dp, n_ctx, queries, grad_out, out_weight, residues):
    chans, columns = out_weight.shape
    return (
        n_ctx == 8
        and n_dp >= 4
        and n_dp % 2 == 0
        and queries.shape[0] == n_dp
        and queries.shape[1] == n_ctx * LANES
        and chans % (n_ctx * 16) == 0
        and chans % LANES == 0
        and columns % (n_ctx * n_dp * LANES) == 0
        and residues.shape[1] % 16 == 0
        and 2 * residues.shape[1] <= LANES
        and chans <= 512
        and columns <= 8192
    )


def solution(mesh):
    placed = (
        P("dp", "ctx", None),
        P("dp", "ctx", None),
        P("dp", "ctx", None),
        P("dp", "ctx", None),
        P(None, "ctx"),
        P("ctx", None),
        P("ctx", None),
    )
    n_dp, n_ctx = mesh.shape["dp"], mesh.shape["ctx"]

    outputs = (
        P("dp", None, "ctx"),
        P("dp", None, "ctx"),
        P("dp", None, "ctx"),
        P(None, "ctx"),
        P("ctx", None),
        P("ctx", None),
    )

    def run(queries, keys, values, grad_out, out_weight, residues, decays):
        inner = body
        if fits_fused(n_dp, n_ctx, queries, grad_out, out_weight, residues):
            inner = functools.partial(fused_body, n_dp, n_ctx)
        mapped = jax.shard_map(inner, mesh=mesh, in_specs=placed, out_specs=outputs, check_vma=False)
        return mapped(queries, keys, values, grad_out, out_weight, residues, decays)

    return run
```

```python
import functools
import math

import jax
import jax.numpy as jnp
from jax import lax
from jax.experimental import pallas as pl
from jax.experimental.pallas import tpu as pltpu
from jax.sharding import PartitionSpec as P

FFT_COLS = 128


HIGHEST = lax.Precision.HIGHEST


def fourier_tables(fft_rows, fft_cols):
    total = fft_rows * fft_cols
    row_index = jnp.arange(fft_rows, dtype=jnp.int32)
    col_index = jnp.arange(fft_cols, dtype=jnp.int32)
    first = (row_index[:, None] * row_index[None, :] % fft_rows).astype(jnp.float32) * (
        2.0 * math.pi / fft_rows
    )
    twist = (row_index[:, None] * col_index[None, :] % total).astype(jnp.float32) * (
        2.0 * math.pi / total
    )
    second = (col_index[:, None] * col_index[None, :] % fft_cols).astype(jnp.float32) * (
        2.0 * math.pi / fft_cols
    )
    return (
        (jnp.cos(first), -jnp.sin(first)),
        (jnp.cos(twist), -jnp.sin(twist)),
        (jnp.cos(second), -jnp.sin(second)),
    )


def complex_product(left_re, left_im, right_re, right_im):
    return (left_re * right_re - left_im * right_im, left_re * right_im + left_im * right_re)


def apply_middle(table_re, table_im, data_re):

    def single(table, data):
        return jnp.einsum("kn,cnm->ckm", table, data, precision=HIGHEST)

    return (single(table_re, data_re), single(table_im, data_re))


def apply_last(table_re, table_im, data_re, data_im):

    def single(data, table):
        return jnp.einsum("ckm,mj->ckj", data, table, precision=HIGHEST)

    return (
        single(data_re, table_re) - single(data_im, table_im),
        single(data_im, table_re) + single(data_re, table_im),
    )


def forward_transform(signal, tables):
    (first_re, first_im), (twist_re, twist_im), (second_re, second_im) = tables
    section_re, section_im = apply_middle(first_re, first_im, signal)
    section_re, section_im = complex_product(section_re, section_im, twist_re, twist_im)
    return apply_last(second_re, second_im, section_re, section_im)


def inverse_transform(spec_re, spec_im, tables):
    (first_re, first_im), (twist_re, twist_im), (second_re, second_im) = tables
    section_re, section_im = apply_last(second_re, -second_im, spec_re, spec_im)
    section_re, section_im = complex_product(section_re, section_im, twist_re, -twist_im)
    result = jnp.einsum("kn,cnm->ckm", first_re, section_re, precision=HIGHEST) + jnp.einsum(
        "kn,cnm->ckm", first_im, section_im, precision=HIGHEST
    )
    total = first_re.shape[0] * second_re.shape[0]
    return result / float(total)


def padded_grid(signal, fft_rows, fft_cols):
    channels, seq_len = signal.shape
    padded = jnp.concatenate(
        [signal, jnp.zeros((channels, fft_rows * fft_cols - seq_len), jnp.float32)], axis=1
    )
    return padded.reshape(channels, fft_rows, fft_cols)


def leading_part(grid, seq_len):
    return grid.reshape(grid.shape[0], -1)[:, :seq_len]


def channels_first(block):
    return block[0].astype(jnp.float32).T


def rounded_sum(terms):
    rounded = lax.optimization_barrier(terms.astype(jnp.bfloat16))
    return jnp.sum(rounded.astype(jnp.float32), axis=0)


def body(queries, keys, values, grad_out, out_weight, residues, decays):
    channels = out_weight.shape[0]
    block_width = out_weight.shape[1]
    tok_rows = grad_out.shape[1]
    grad_cols = lax.all_to_all(grad_out, "ctx", split_axis=2, concat_axis=1, tiled=True)
    shard_piece = lax.all_gather(out_weight, "ctx", axis=1, tiled=True)
    blocks = shard_piece.shape[1] // block_width
    partial_value = grad_out[0]
    partial_value = partial_value.reshape(tok_rows, blocks, block_width)
    weight_part = shard_piece.reshape(channels, blocks, block_width)
    terms = jnp.einsum(
        "tks,cks->ktc", partial_value, weight_part, preferred_element_type=jnp.float32
    )
    gated_sum = rounded_sum(terms)
    grad_gated = gated_sum.astype(jnp.bfloat16)[None]
    query_ch, key_ch, value_ch, gated_grad_ch = (
        lax.all_to_all(queries, "ctx", split_axis=2, concat_axis=1, tiled=True),
        lax.all_to_all(keys, "ctx", split_axis=2, concat_axis=1, tiled=True),
        lax.all_to_all(values, "ctx", split_axis=2, concat_axis=1, tiled=True),
        lax.all_to_all(grad_gated, "ctx", split_axis=2, concat_axis=1, tiled=True),
    )
    grad_gated_full = channels_first(gated_grad_ch)
    seq_len = query_ch.shape[1]
    fft_rows = 2 * seq_len // FFT_COLS
    tables = fourier_tables(fft_rows, FFT_COLS)
    query_full = channels_first(query_ch)
    key_full = channels_first(key_ch)
    value_full = channels_first(value_ch)
    positions = jnp.arange(seq_len).astype(jnp.float32)
    decay_terms = jnp.exp(-decays[:, :, None] * positions[None, None, :])
    filter_taps = jnp.sum(residues[:, :, None] * decay_terms, axis=1)
    product = key_full * value_full
    grad_conv = grad_gated_full * query_full
    prod_re, prod_im = forward_transform(padded_grid(product, fft_rows, FFT_COLS), tables)
    taps_re, taps_im = forward_transform(padded_grid(filter_taps, fft_rows, FFT_COLS), tables)
    grad_re, grad_im = forward_transform(padded_grid(grad_conv, fft_rows, FFT_COLS), tables)
    conv_out = leading_part(
        inverse_transform(*complex_product(prod_re, prod_im, taps_re, taps_im), tables), seq_len
    )
    grad_product = leading_part(
        inverse_transform(*complex_product(taps_re, -taps_im, grad_re, grad_im), tables), seq_len
    )
    grad_taps = leading_part(
        inverse_transform(*complex_product(prod_re, -prod_im, grad_re, grad_im), tables), seq_len
    )
    gated = (query_full * conv_out).T.astype(jnp.bfloat16)[None]
    grad_queries = (grad_gated_full * conv_out).T.astype(jnp.bfloat16)[None]
    grad_keys = (grad_product * value_full).T.astype(jnp.bfloat16)[None]
    grad_values = (grad_product * key_full).T.astype(jnp.bfloat16)[None]
    partial_value = lax.dot_general(
        lax.all_gather(gated, "ctx", axis=2, tiled=True)[0],
        grad_cols[0],
        (((0,), (0,)), ((), ())),
        preferred_element_type=jnp.float32,
    )
    grad_weight = partial_value
    grad_residues = jnp.sum(grad_taps[:, None, :] * decay_terms, axis=2)
    grad_decays = -residues * jnp.sum(
        (grad_taps * positions[None, :])[:, None, :] * decay_terms, axis=2
    )
    grad_weight, grad_residues, grad_decays = (
        lax.psum(grad_weight.astype(jnp.bfloat16), "dp").astype(jnp.float32),
        lax.psum(grad_residues.astype(jnp.bfloat16), "dp").astype(jnp.float32),
        lax.psum(grad_decays.astype(jnp.bfloat16), "dp").astype(jnp.float32),
    )
    return (grad_queries, grad_keys, grad_values, grad_weight, grad_residues, grad_decays)

LANES = 128
PARTS = 4
MESH = pl.DeviceIdType.MESH
F32 = jnp.float32
BF16 = jnp.bfloat16


def dot_nt(left, right):
    return lax.dot_general(left, right, (((1,), (1,)), ((), ())), preferred_element_type=F32)


def split_rows(data):
    high = data.astype(BF16)
    low = (data - high.astype(F32)).astype(BF16)
    return jnp.concatenate([high, low], axis=0)


def fused_kernel(
    n_dp, n_ctx,
    q_ref, k_ref, v_ref, go_ref, w_ref, dec_ref, res_ref,
    gq_ref, gk_ref, gv_ref, dw_ref, par_res_ref, par_dec_ref,
    qkv_send, qkv_recv, gcols, wbuf, toep, etab, utab, vtab, cmat, bmat, dec_wide, res_wide,
    prod, conv, gconv, gprod, ubuf, sbuf, vbuf, zbuf,
    gat_send, gat_all, gg_acc, gg_send, gg_recv, ggt_send, ggt_recv,
    dwp, dwy, dwz, dwf, red, red_send, red_recv,
    q_ss, q_rs, g_ss, g_rs, w_ss, w_rs, a_ss, a_rs, b_ss, b_rs, c_ss, c_rs, t_ss, t_rs,
    y_ss, y_rs, z_ss, z_rs, f_ss, f_rs, r_ss, r_rs, loc_sem,
):
    me_d = lax.axis_index("dp")
    me_c = lax.axis_index("ctx")
    chans = q_ref.shape[2]
    mine = chans // n_ctx
    width = gcols.shape[2]
    order = dec_ref.shape[0]
    block_rows = chans // PARTS
    half = n_ctx // 2
    side = lax.rem(me_c, 2)
    partner = me_c + 1 - 2 * side
    ctx_peers = [lax.rem(me_c + s, n_ctx) for s in range(1, n_ctx)]
    dp_peers = [lax.rem(me_d + s, n_dp) for s in range(1, n_dp)]
    sibling = me_d + 1 - 2 * lax.rem(me_d, 2)
    far_peers = [lax.rem(me_d + 2 * s, n_dp) for s in range(1, n_dp // 2)]
    far_sources = [lax.rem(me_d + n_dp - 2 * s, n_dp) for s in range(1, n_dp // 2)]
    line_peers = [lax.rem(me_c + 2 * s, n_ctx) for s in range(1, half)]

    def remote(src, dst, ss, rs, **to):
        return pltpu.make_async_remote_copy(
            src_ref=src, dst_ref=dst, send_sem=ss, recv_sem=rs, device_id=to, device_id_type=MESH
        )

    def rows(index, size):
        return pl.ds(pl.multiple_of(index * size, size), size)

    barrier = pltpu.get_barrier_semaphore()
    for peer in ctx_peers:
        pl.semaphore_signal(barrier, inc=1, device_id={"ctx": peer}, device_id_type=MESH)
    for peer in dp_peers:
        pl.semaphore_signal(barrier, inc=1, device_id={"dp": peer}, device_id_type=MESH)

    for part, ref in enumerate((q_ref, k_ref, v_ref)):
        for at in range(0, chans, LANES):
            qkv_send[part, at : at + LANES, :] = ref[0, :, at : at + LANES].astype(F32).T.astype(BF16)
    pl.semaphore_wait(barrier, n_ctx - 1 + n_dp - 1)

    q_copies = [
        remote(qkv_send.at[:, rows(peer, mine), :], qkv_recv.at[me_c], q_ss.at[i], q_rs.at[i], ctx=peer)
        for i, peer in enumerate(ctx_peers)
    ]
    for copy in q_copies:
        copy.start()
    qkv_recv[me_c] = qkv_send[:, rows(me_c, mine), :]

    def cols_copy(i, peer, k):
        return remote(
            go_ref.at[0, :, rows(k * n_dp + peer, width)],
            gcols.at[k, rows(me_d, LANES), :],
            g_ss.at[i, k], g_rs.at[i, k], dp=peer,
        )

    def cols_own(k):
        return pltpu.make_async_copy(
            go_ref.at[0, :, rows(k * n_dp + me_d, width)], gcols.at[k, rows(me_d, LANES), :], loc_sem.at[k]
        )

    for k in range(n_ctx):
        for i, peer in enumerate(dp_peers):
            cols_copy(i, peer, k).start()
        cols_own(k).start()

    own_w = pltpu.make_async_copy(w_ref.at[:, rows(me_d, width)], wbuf.at[me_c], loc_sem.at[n_ctx])
    own_w.start()
    w_own = w_ref.at[:, rows(me_d, width)]
    w_copies = [
        remote(w_own, wbuf.at[me_c], w_ss.at[i], w_rs.at[i], ctx=peer)
        for i, peer in enumerate(line_peers + [partner])
    ]
    w_copies[half - 1].start()

    lane = lax.broadcasted_iota(jnp.int32, (order, LANES), 1).astype(F32)
    upper = lax.broadcasted_iota(jnp.int32, (LANES, LANES), 1) >= lax.broadcasted_iota(
        jnp.int32, (LANES, LANES), 0
    )
    column = lax.broadcasted_iota(jnp.int32, (mine, LANES), 1)
    rates, weights = dec_ref[...], res_ref[...]
    for c in range(mine):
        dec_wide[c] = jnp.broadcast_to(rates[:, c : c + 1], (order, LANES))
        res_wide[c] = jnp.broadcast_to(weights[:, c : c + 1], (order, LANES))
    rate_rows, weight_rows = rates.T, weights.T
    rest = jnp.zeros((mine, LANES - 2 * order), F32)
    fade = jnp.exp(-float(LANES) * jnp.concatenate([rate_rows, rate_rows, rest], axis=1))
    step = jnp.where((column >= order) & (column < 2 * order), float(LANES), 0.0)
    weight_rows = jnp.concatenate([weight_rows, jnp.zeros((mine, LANES - order), F32)], axis=1)
    blank = jnp.zeros((LANES - 2 * order, LANES), F32)

    def tables(c, carry):
        rate = dec_wide[c]
        weight = res_wide[c]
        value = jnp.exp(-rate * lane)
        etab[c] = jnp.concatenate([split_rows(value), split_rows(value * lane)], axis=0)
        after = jnp.exp(-rate * (lane + 1.0))
        before = jnp.exp(-rate * (LANES - 1.0 - lane))
        cmat[c] = (weight * after).astype(BF16)
        bmat[c] = before.astype(BF16)
        vtab[c] = jnp.concatenate([after, after * (lane + 1.0), blank], axis=0).astype(BF16)
        utab[c] = jnp.concatenate([before, before * (LANES - 1.0 - lane), blank], axis=0).astype(BF16)
        taps = jnp.sum(weight * value, axis=0, keepdims=True)
        rolled = pltpu.roll(jnp.broadcast_to(taps, (LANES, LANES)), 0, 1, stride=1, stride_axis=0)
        toep[c] = jnp.where(upper, rolled, 0.0).astype(BF16)
        return carry

    lax.fori_loop(0, mine, tables, 0, unroll=4)

    def channel(ref, c):
        return ref[pl.ds(c, n_ctx, stride=mine), :]

    def joined(both):
        return both[:n_ctx] + both[n_ctx:]

    for copy in q_copies:
        copy.wait()
    for copy in w_copies[: half - 1]:
        copy.start()
    for j in range(n_ctx):
        prod[j * mine : (j + 1) * mine, :] = qkv_recv[j, 1].astype(F32) * qkv_recv[j, 2].astype(F32)

    def enter(c, carry):
        ubuf[pl.ds(c, n_ctx, stride=mine), :] = joined(dot_nt(split_rows(channel(prod, c)), utab[c]))
        return carry

    lax.fori_loop(0, mine, enter, 0, unroll=8)
    state = jnp.zeros((mine, LANES), F32)
    for j in range(n_ctx):
        part = slice(j * mine, (j + 1) * mine)
        sbuf[part, :] = state
        state = fade * (state + step * pltpu.roll(state, order, 1)) + ubuf[part, :]

    def forward(c, carry):
        near = jnp.dot(split_rows(channel(prod, c)), toep[c], preferred_element_type=F32)
        far = jnp.dot(split_rows(channel(sbuf, c))[:, :order], cmat[c], preferred_element_type=F32)
        conv[pl.ds(c, n_ctx, stride=mine), :] = joined(near + far)
        return carry

    lax.fori_loop(0, mine, forward, 0, unroll=8)

    for j in range(n_ctx):
        gat_send[j] = (qkv_recv[j, 0].astype(F32) * conv[j * mine : (j + 1) * mine, :]).astype(BF16)
    a_copies = [
        remote(
            gat_send.at[peer],
            gat_all.at[rows(me_c, mine), rows(me_d, LANES)],
            a_ss.at[i], a_rs.at[i], ctx=peer,
        )
        for i, peer in enumerate(ctx_peers)
    ]
    for copy in a_copies:
        copy.start()
    gat_all[rows(me_c, mine), rows(me_d, LANES)] = gat_send[me_c]

    for copy in a_copies:
        copy.wait()
    b_copies = [
        remote(
            gat_all.at[:, rows(me_d, LANES)], gat_all.at[:, rows(me_d, LANES)],
            b_ss.at[i], b_rs.at[i], dp=peer,
        )
        for i, peer in enumerate(far_peers + [sibling])
    ]
    for copy in b_copies:
        copy.start()

    forwards = []

    def forward_weights(i):
        w_copies[i].wait()
        source = lax.rem(me_c + n_ctx - 2 * (i + 1), n_ctx)
        copy = remote(wbuf.at[source], wbuf.at[source], w_ss.at[half + i], w_rs.at[half + i], ctx=partner)
        copy.start()
        forwards.append(copy)

    forward_weights(0)
    for i, source in enumerate(far_sources):
        b_copies[i].wait()
        copy = remote(
            gat_all.at[:, rows(source, LANES)], gat_all.at[:, rows(source, LANES)],
            b_ss.at[n_dp // 2 + i], b_rs.at[n_dp // 2 + i], dp=sibling,
        )
        copy.start()
        b_copies.append(copy)
    for copy in b_copies[n_dp // 2 - 1 :]:
        copy.wait()
    for k in range(n_ctx):
        for i, peer in enumerate(dp_peers):
            cols_copy(i, peer, k).wait()
        cols_own(k).wait()

    def weight_block(k, h):
        part = slice(h * block_rows, (h + 1) * block_rows)
        dwp[k, part, :] = jnp.dot(gat_all[part, :], gcols[k], preferred_element_type=F32).astype(BF16)

    def part_of(h):
        return slice(h * block_rows, (h + 1) * block_rows)

    line = me_c // 2
    y_copies = {}
    for h in range(PARTS):
        for s in list(range(1, half)) + [0]:
            k = 2 * lax.rem(line + s, half) + 1 - side
            weight_block(k, h)
            copy = remote(
                dwp.at[k, part_of(h), :], dwy.at[s, part_of(h), :], y_ss.at[h, s], y_rs.at[h, s], ctx=partner
            )
            copy.start()
            y_copies[h, s] = copy
        if h + 1 < half - 1:
            forward_weights(h + 1)

    def own_blocks(z, carry):
        for h in range(PARTS):
            weight_block(2 * z + side, h)
        return carry

    lax.fori_loop(0, half, own_blocks, 0)

    z_copies = {}

    def pass_on(h):
        part = part_of(h)
        for i, peer in enumerate(line_peers):
            y_copies[h, i + 1].wait()
            dwp[peer, part, :] = (dwp[peer, part, :].astype(F32) + dwy[i + 1, part, :].astype(F32)).astype(BF16)
            copy = remote(
                dwp.at[peer, part, :], dwz.at[i, part, :], z_ss.at[h, i], z_rs.at[h, i], ctx=peer
            )
            copy.start()
            z_copies[h, i] = copy

    def finish(h):
        part = part_of(h)
        for i in range(half - 1):
            z_copies[h, i].wait()
        y_copies[h, 0].wait()
        last = dwp[me_c, part, :].astype(F32) + dwy[0, part, :].astype(F32)
        for i in range(half - 1):
            last = last + dwz[i, part, :].astype(F32)
        dwf[part, rows(me_d, width)] = last.astype(BF16)
        copies = [
            remote(
                dwf.at[part, rows(me_d, width)], dwf.at[part, rows(me_d, width)],
                f_ss.at[h, i], f_rs.at[h, i], dp=peer,
            )
            for i, peer in enumerate(far_peers + [sibling])
        ]
        for copy in copies:
            copy.start()
        return copies

    def share(h):
        part = part_of(h)
        for i, source in enumerate(far_sources):
            f_copies[h][i].wait()
            copy = remote(
                dwf.at[part, rows(source, width)], dwf.at[part, rows(source, width)],
                f_ss.at[h, n_dp // 2 + i], f_rs.at[h, n_dp // 2 + i], dp=sibling,
            )
            copy.start()
            f_copies[h].append(copy)

    pass_on(0)
    own_w.wait()
    w_copies[half - 1].wait()
    for copy in forwards:
        copy.wait()
    gg_acc[...] = jnp.zeros_like(gg_acc)

    def terms(k, carry):
        gg_acc[...] += dot_nt(wbuf[k], gcols[k])
        return carry

    lax.fori_loop(0, n_ctx, terms, 0)
    gg_send[...] = gg_acc[...].astype(BF16)
    c_copies = [
        remote(gg_send.at[:, rows(peer, LANES)], gg_recv.at[me_d], c_ss.at[i], c_rs.at[i], dp=peer)
        for i, peer in enumerate(dp_peers)
    ]
    for copy in c_copies:
        copy.start()
    gg_recv[me_d] = gg_send[:, rows(me_d, LANES)]
    pass_on(1)

    for copy in c_copies:
        copy.wait()
    total = gg_recv[0].astype(F32)
    for d in range(1, n_dp):
        total = total + gg_recv[d].astype(F32)
    ggt_send[...] = total.astype(BF16)
    t_copies = [
        remote(ggt_send.at[rows(peer, mine), :], ggt_recv.at[me_c], t_ss.at[i], t_rs.at[i], ctx=peer)
        for i, peer in enumerate(ctx_peers)
    ]
    for copy in t_copies:
        copy.start()
    ggt_recv[me_c] = ggt_send[rows(me_c, mine), :]
    pass_on(2)
    f_copies = [finish(0)]
    pass_on(3)

    for copy in t_copies:
        copy.wait()
    for j in range(n_ctx):
        part = slice(j * mine, (j + 1) * mine)
        gated_grad = ggt_recv[j].astype(F32)
        gconv[part, :] = gated_grad * qkv_recv[j, 0].astype(F32)
        gq_ref[:, j * LANES : (j + 1) * LANES] = (gated_grad * conv[part, :]).astype(BF16)

    def leave(c, carry):
        vbuf[pl.ds(c, n_ctx, stride=mine), :] = joined(dot_nt(split_rows(channel(gconv, c)), vtab[c]))
        return carry

    lax.fori_loop(0, mine, leave, 0, unroll=8)
    state = jnp.zeros((mine, LANES), F32)
    plain_sum, timed_sum = state, state
    for j in reversed(range(n_ctx)):
        part = slice(j * mine, (j + 1) * mine)
        zbuf[part, :] = state
        left, right = vbuf[part, :], sbuf[part, :]
        state = fade * state + weight_rows * left
        plain_sum = plain_sum + left * right
        timed_sum = timed_sum + left * pltpu.roll(right, order, 1) + pltpu.roll(left, order, 1) * right
    far_sums = jnp.where(column < order, plain_sum, jnp.where(column < 2 * order, timed_sum, 0.0))

    def backward(c, carry):
        near = dot_nt(split_rows(channel(gconv, c)), toep[c])
        far = jnp.dot(split_rows(channel(zbuf, c))[:, :order], bmat[c], preferred_element_type=F32)
        gprod[pl.ds(c, n_ctx, stride=mine), :] = joined(near + far)
        return carry

    def lags(c, carry):
        outer = lax.dot_general(
            channel(prod, c).astype(BF16), channel(gconv, c).astype(BF16),
            (((0,), (0,)), ((), ())), preferred_element_type=F32,
        )
        sums = dot_nt(etab[c], jnp.where(upper, outer, 0.0).astype(BF16))
        plain = sums[0:order] + sums[order : 2 * order]
        timed = sums[2 * order : 3 * order] + sums[3 * order :]
        grown = jnp.exp(dec_wide[c] * lane)
        red[c, 0:order, :] = plain * grown
        red[c, order:, :] = (timed - lane * plain) * grown
        return carry

    f_copies.append(finish(1))
    share(0)
    lax.fori_loop(0, mine, lags, 0, unroll=4)
    f_copies.append(finish(2))
    share(1)
    sums = jnp.sum(red[...], axis=2)
    sums = jnp.concatenate([sums, rest], axis=1) + far_sums
    red_send[...] = jnp.where(column < order, sums, -pltpu.roll(weight_rows, order, 1) * sums)
    r_copies = [
        remote(red_send, red_recv.at[me_d], r_ss.at[i], r_rs.at[i], dp=peer)
        for i, peer in enumerate(dp_peers)
    ]
    for copy in r_copies:
        copy.start()
    red_recv[me_d] = red_send[...]
    lax.fori_loop(0, mine, backward, 0, unroll=8)
    f_copies.append(finish(3))
    share(2)
    for j in range(n_ctx):
        part = slice(j * mine, (j + 1) * mine)
        at = slice(j * LANES, (j + 1) * LANES)
        gk_ref[:, at] = (gprod[part, :] * qkv_recv[j, 2].astype(F32)).astype(BF16)
        gv_ref[:, at] = (gprod[part, :] * qkv_recv[j, 1].astype(F32)).astype(BF16)
    share(3)
    for copy in r_copies:
        copy.wait()
    total = red_recv[0]
    for d in range(1, n_dp):
        total = total + red_recv[d]
    turned = total.T
    par_res_ref[...] = turned[0:order, :]
    par_dec_ref[...] = turned[order : 2 * order, :]
    for copies in f_copies:
        for copy in copies[n_dp // 2 - 1 :]:
            copy.wait()
    dw_ref[...] = dwf[...]


def fused_body(n_dp, n_ctx, queries, keys, values, grad_out, out_weight, residues, decays):
    chans, block = out_weight.shape
    mine, order = residues.shape
    width = block // n_dp
    vm = pl.BlockSpec(memory_space=pltpu.VMEM)
    hbm = pl.BlockSpec(memory_space=pl.ANY)
    sem = pltpu.SemaphoreType.DMA
    n_c, n_d, half = n_ctx - 1, n_dp - 1, n_ctx // 2

    def twice(*shape):
        return [sem(shape), sem(shape)]

    scratch = [
        pltpu.VMEM((3, chans, LANES), BF16),
        pltpu.VMEM((n_ctx, 3, mine, LANES), BF16),
        pltpu.VMEM((n_ctx, n_dp * LANES, width), BF16),
        pltpu.VMEM((n_ctx, chans, width), BF16),
        pltpu.VMEM((mine, LANES, LANES), BF16),
        pltpu.VMEM((mine, 4 * order, LANES), BF16),
        pltpu.VMEM((mine, LANES, LANES), BF16),
        pltpu.VMEM((mine, LANES, LANES), BF16),
        pltpu.VMEM((mine, order, LANES), BF16),
        pltpu.VMEM((mine, order, LANES), BF16),
        pltpu.VMEM((mine, order, LANES), F32),
        pltpu.VMEM((mine, order, LANES), F32),
        pltpu.VMEM((chans, LANES), F32),
        pltpu.VMEM((chans, LANES), F32),
        pltpu.VMEM((chans, LANES), F32),
        pltpu.VMEM((chans, LANES), F32),
        pltpu.VMEM((chans, LANES), F32),
        pltpu.VMEM((chans, LANES), F32),
        pltpu.VMEM((chans, LANES), F32),
        pltpu.VMEM((chans, LANES), F32),
        pltpu.VMEM((n_ctx, mine, LANES), BF16),
        pltpu.VMEM((chans, n_dp * LANES), BF16),
        pltpu.VMEM((chans, n_dp * LANES), F32),
        pltpu.VMEM((chans, n_dp * LANES), BF16),
        pltpu.VMEM((n_dp, chans, LANES), BF16),
        pltpu.VMEM((chans, LANES), BF16),
        pltpu.VMEM((n_ctx, mine, LANES), BF16),
        pltpu.VMEM((n_ctx, chans, width), BF16),
        pltpu.VMEM((half, chans, width), BF16),
        pltpu.VMEM((half - 1, chans, width), BF16),
        pltpu.VMEM((chans, block), BF16),
        pltpu.VMEM((mine, 2 * order, LANES), F32),
        pltpu.VMEM((mine, LANES), F32),
        pltpu.VMEM((n_dp, mine, LANES), F32),
    ]
    scratch += twice(n_c) + twice(n_d, n_ctx) + twice(n_c) + twice(n_c) + twice(n_d) + twice(n_d)
    scratch += twice(n_c) + twice(PARTS, half) + twice(PARTS, half - 1) + twice(PARTS, n_d) + twice(n_d) + [sem((n_ctx + 1,))]
    blocks = jax.ShapeDtypeStruct((mine, n_ctx * LANES), BF16)
    params = jax.ShapeDtypeStruct((order, mine), F32)
    gq, gk, gv, dw, par_res, par_dec = pl.pallas_call(
        functools.partial(fused_kernel, n_dp, n_ctx),
        out_shape=(
            blocks, blocks, blocks,
            jax.ShapeDtypeStruct((chans, block), BF16),
            params, params,
        ),
        in_specs=[vm, vm, vm, hbm, hbm, vm, vm],
        out_specs=(vm,) * 6,
        scratch_shapes=scratch,
        compiler_params=pltpu.CompilerParams(
            collective_id=0, has_side_effects=True, vmem_limit_bytes=58 * 1024 * 1024
        ),
        cost_estimate=pl.CostEstimate(flops=6 * 10**9, bytes_accessed=8 * 2**20, transcendentals=2**20),
    )(
        queries, keys, values, grad_out, out_weight,
        decays.T, residues.T,
    )

    def positions_first(grid):
        return grid.T[None]

    return (
        positions_first(gq), positions_first(gk), positions_first(gv),
        dw.astype(F32), par_res.T, par_dec.T,
    )


def fits_fused(n_dp, n_ctx, queries, grad_out, out_weight, residues):
    chans, columns = out_weight.shape
    return (
        n_ctx == 8
        and n_dp >= 4
        and n_dp % 2 == 0
        and queries.shape[0] == n_dp
        and queries.shape[1] == n_ctx * LANES
        and chans % (n_ctx * 16) == 0
        and chans % LANES == 0
        and columns % (n_ctx * n_dp * LANES) == 0
        and residues.shape[1] % 16 == 0
        and 2 * residues.shape[1] <= LANES
        and chans <= 512
        and columns <= 8192
    )


def solution(mesh):
    placed = (
        P("dp", "ctx", None),
        P("dp", "ctx", None),
        P("dp", "ctx", None),
        P("dp", "ctx", None),
        P(None, "ctx"),
        P("ctx", None),
        P("ctx", None),
    )
    n_dp, n_ctx = mesh.shape["dp"], mesh.shape["ctx"]

    outputs = (
        P("dp", None, "ctx"),
        P("dp", None, "ctx"),
        P("dp", None, "ctx"),
        P(None, "ctx"),
        P("ctx", None),
        P("ctx", None),
    )

    def run(queries, keys, values, grad_out, out_weight, residues, decays):
        inner = body
        if fits_fused(n_dp, n_ctx, queries, grad_out, out_weight, residues):
            inner = functools.partial(fused_body, n_dp, n_ctx)
        mapped = jax.shard_map(inner, mesh=mesh, in_specs=placed, out_specs=outputs, check_vma=False)
        return mapped(queries, keys, values, grad_out, out_weight, residues, decays)

    return run
```
